32 devices in a mesh: gx: 16 (over z, y, core), gy: 2 (over x).
Axes of the slice: x: 2, y: 2, z: 4, core: 2. Of those that a mesh axis runs over, the one named last changes fastest.
Arguments:
- velocity: float32 [128, 64, 256], P('gx', 'gy'), may hold values from 1.5 to 4.5
- density: float32 [128, 64, 256], P('gx', 'gy'), may hold values from 1.8 to 2.6
- adjoint_last: float32 [128, 64, 256], P('gx', 'gy'), may hold values from -6 to 6
- adjoint_now: float32 [128, 64, 256], P('gx', 'gy'), may hold values from -6 to 6
- forward_accel: bfloat16 [8, 128, 64, 256], P(None, 'gx', 'gy'), may hold values from -6 to 6
- residual_panels: bfloat16 [16384, 128], P(('gx', 'gy')), may hold values from -6 to 6
- owner_slab: int32 [16384, 1], P(('gx', 'gy')), may hold values from 0 to 15; in each aligned block of 512 rows (0 to 511, 512 to 1023, ...) at most 32 rows name the same one
- receiver_cell: int32 [16384], P(('gx', 'gy')), may hold values from 0 to 65535
- trace_offset: int32 [16384], P(('gx', 'gy')), may hold values from 0 to 31
Outputs:
- sensitivity: float32 [64, 128, 32], P('gx', 'gy')
- adjoint_final: float32 [128, 64, 256], P('gx', 'gy')
The draws below stay inside these ranges and needn't reach their ends.
Inputs may be any that keep to these rules, and one draw needn't show every extreme that they name: `owner_slab`: the rows of one device name one slab at most 32 times, a bound that some block reaches. `receiver_cell`: numbered (x * 32 + y) * 256 + z within the owner's block.
All inputs are finite; a program needn't handle non-finite values.
Results may differ from the reference program's by a relative error of at most 0.0003.
Values may be sent and summed in bfloat16 or wider, within the bound.
No kernel may reach another device: no remote copies, remote signals or barrier semaphores. Data moves between devices by JAX's collectives and lax.ppermute only.
A program may use at most 64 MiB of HBM per device.

```python
import math
import jax
import jax.numpy as jnp
import numpy as np

CX = 8
CY = 32
NZ = 256
SENS_DEV = 512
PANEL = 128
STEPS = 8
CAP = 32
NX = 128
NY = 64
SENSORS = 16384
N_GX = 16
N_GY = 2


def plant(result, rng, low, high):
    dims = result.shape
    index_at = [jax.random.randint(jax.random.fold_in(rng, axis), (), 0, dims[axis]) for axis in range(len(dims))]
    result = result.at[tuple(index_at)].set(low)
    longest = dims.index(max(dims))
    index_at[longest] = (index_at[longest] + 1) % dims[longest]
    return result.at[tuple(index_at)].set(high)


def steps_of(own_key, shape, cuts, low, high):
    factor_of, own = 1.0, jax.random.fold_in(own_key, 6)
    for axis_at, parts in cuts:
        draws = jnp.exp(jax.random.uniform(jax.random.fold_in(own, axis_at), (parts,), jnp.float32, low / len(cuts), high / len(cuts)))
        factor_of = factor_of * jnp.repeat(draws, shape[axis_at] // parts).reshape([-1 if axis == axis_at else 1 for axis in range(len(shape))])
    return factor_of


def shared_out(own_key, own, number, rows, count, top, most, skew):
    ranking = jax.random.permutation(own_key, count)
    crowded, ordinary = shares(count, rows * top, most, skew, True), shares(count, rows * top, most, skew, False)
    places = jnp.arange(count)

    def named(sizes, turn):
        used = int((sizes > 0).sum())
        fixed = max(1, used // 4)
        shifted = fixed + (places - fixed + turn * (used - fixed)) % max(1, count - fixed)
        return jnp.zeros((count,), jnp.int32).at[ranking[jnp.where(places < fixed, places, shifted)]].set(jnp.asarray(sizes, jnp.int32))

    sizes = jnp.where(number % 4 == 0, named(crowded, number // 4), named(ordinary, number - number // 4 - 1))
    mixed = jax.random.permutation(jax.random.fold_in(own, 3), count)
    source_of, receiver = mixed[0:count // 2 * 2:2], mixed[1:count // 2 * 2:2]
    slack = jnp.minimum(sizes[source_of] - 1, most - sizes[receiver]) // 2
    slack = jnp.where((source_of == ranking[0]) | (receiver == ranking[0]) | (sizes[receiver] == 0), 0, jnp.maximum(slack, 0))
    shifted = jax.random.randint(jax.random.fold_in(own, 4), (count // 2,), 0, 1 << 20) % (slack + 1)
    sizes = sizes.at[source_of].add(-shifted).at[receiver].add(shifted)
    items = jnp.searchsorted(jnp.cumsum(sizes), jnp.arange(rows * top), side="right").astype(jnp.int32)
    table = items.reshape(top, rows).T
    table = table[jax.random.permutation(jax.random.fold_in(own, 1), rows)]
    turn = jax.random.randint(jax.random.fold_in(own, 2), (rows, 1), 0, top)
    return jnp.take_along_axis(table, (jnp.arange(top)[None, :] + turn) % top, axis=1)


def shares(number_of, total, reach, lean, full):
    weights = [(1 << 20) // math.isqrt(rank ** lean) + 1 for rank in range(1, number_of + 1)]
    largest = reach if full else min(reach, max(-(-total // number_of), total * weights[0] // sum(weights)))
    least = 1 if total - largest >= number_of - 1 else 0
    counts, surplus = [largest] + [least] * (number_of - 1), total - largest - least * (number_of - 1)
    while surplus > 0:
        candidates = [i for i in range(1, number_of) if counts[i] < largest] or [i for i in range(1, number_of) if counts[i] < reach]
        mass, remaining = sum([weights[i] for i in candidates]), surplus
        for i in candidates:
            more = min(reach - counts[i], max(1, remaining * weights[i] // mass), surplus)
            counts[i] = counts[i] + more
            surplus = surplus - more
    return np.array(counts)


def centred(stream_key, shape, width, limit, cuts=(), kind=jnp.bfloat16):
    values = width * jax.random.normal(stream_key, shape, jnp.float32)
    if cuts:
        values = values * steps_of(stream_key, shape, cuts, -0.22, 0.18)
    return jnp.clip(values, -limit, limit).astype(kind)


def setup_inputs(seed: int = 0) -> dict:
    key_list = jax.random.split(jax.random.key(seed), 10)
    velocity = jnp.clip(1.5 + 3.0 * jax.random.uniform(key_list[0], (NX, NY, NZ), jnp.float32) ** steps_of(key_list[0], (NX, NY, NZ), ((0, 16), (1, 2)), -0.2, 0.2), 1.5, 4.5)
    density = jnp.clip(1.8 + 0.79999995 * jax.random.uniform(key_list[1], (NX, NY, NZ), jnp.float32) ** steps_of(key_list[1], (NX, NY, NZ), ((0, 16), (1, 2)), -0.2, 0.2), 1.8, 2.6)
    adjoint_last = centred(key_list[2], (NX, NY, NZ), 1.0, 6.0, ((0, 16), (1, 2)), jnp.float32)
    adjoint_now = centred(key_list[3], (NX, NY, NZ), 1.0, 6.0, ((0, 16), (1, 2)), jnp.float32)
    forward_accel = centred(key_list[4], (STEPS, NX, NY, NZ), 1.0, 6.0, ((1, 16), (2, 2)))
    residual_panels = centred(key_list[5], (SENSORS, PANEL), 1.0, 6.0, ((0, 32),))
    owner_slab_keys = jax.random.split(jax.random.fold_in(key_list[6], 1), SENSORS // SENS_DEV)
    owner_slab_turns = jax.random.permutation(jax.random.fold_in(key_list[6], 3), SENSORS // SENS_DEV)
    owner_slab = jax.vmap(lambda own, number: shared_out(jax.random.fold_in(key_list[6], 2), own, number, SENS_DEV, N_GX, 1, CAP, 2))(owner_slab_keys, owner_slab_turns).reshape((SENSORS, 1))
    receiver_cell = plant(jax.random.randint(key_list[7], (SENSORS,), 0, CX * CY * NZ), jax.random.fold_in(key_list[7], 1), 0, (CX * CY * NZ) - 1).astype(jnp.int32)
    trace_offset = plant(jax.random.randint(key_list[8], (SENSORS,), 0, 2 * PANEL // STEPS), jax.random.fold_in(key_list[8], 1), 0, (2 * PANEL // STEPS) - 1).astype(jnp.int32)
    return dict(velocity=velocity, density=density, adjoint_last=adjoint_last, adjoint_now=adjoint_now, forward_accel=forward_accel, residual_panels=residual_panels, owner_slab=owner_slab, receiver_cell=receiver_cell, trace_offset=trace_offset)


def resample(panels, offsets, step_count):
    panel_len = panels.shape[1]
    half_width = panel_len // step_count
    values = panels.astype(jnp.float32)
    clock = (jnp.arange(panel_len, dtype=jnp.int32)[None, :] + offsets[:, None]).astype(jnp.float32)
    columns = []
    for moment in range(step_count):
        weights = jnp.maximum(0.0, 1.0 - jnp.abs(clock - half_width * (moment + 1)) / half_width) * 0.25
        columns.append(jnp.sum(values * weights, axis=1))
    return jnp.stack(columns, axis=1)


def face_list(padded):
    return [padded[2:, 1:-1, 1:-1], padded[:-2, 1:-1, 1:-1],
            padded[1:-1, 2:, 1:-1], padded[1:-1, :-2, 1:-1],
            padded[1:-1, 1:-1, 2:], padded[1:-1, 1:-1, :-2]]


def coarsen(kernel):
    size_a, size_b, size_c = kernel.shape
    blocks = kernel.reshape(size_a // 2, 2, size_b // 2, 2, size_c // 2, 2)
    return jnp.sum(blocks, axis=(1, 3, 5)) * 0.125


def reference(velocity, density, adjoint_last, adjoint_now, forward_accel, residual_panels, owner_slab, receiver_cell, trace_offset):
    sensor_rows = jnp.arange(residual_panels.shape[0], dtype=jnp.int32)
    column_index = (sensor_rows // SENS_DEV) % N_GY
    owners = owner_slab[:, 0]
    local_x = receiver_cell // (CY * NZ)
    local_y = (receiver_cell // NZ) % CY
    local_z = receiver_cell % NZ
    global_cell = ((owners * CX + local_x) * NY + column_index * CY + local_y) * NZ + local_z
    amplitudes = resample(residual_panels, trace_offset, STEPS)
    square = 0.11 * velocity
    stiffness = square * square * density
    rho_pad = jnp.pad(density, 1)
    couplings = [stiffness * (2.0 / (density + nearby)) for nearby in face_list(rho_pad)]
    wave_prev = adjoint_last
    wave = adjoint_now
    accumulated = jnp.zeros(wave.shape, jnp.float32)
    for moment in range(STEPS):
        nearby = face_list(jnp.pad(wave, 1))
        laplace = couplings[0] * (nearby[0] - wave)
        for index in range(1, 6):
            laplace = laplace + couplings[index] * (nearby[index] - wave)
        wave_next = (2.0 * wave - wave_prev) + laplace
        wave_next = wave_next.reshape(-1).at[global_cell].add(amplitudes[:, moment]).reshape(wave.shape)
        accumulated = accumulated + wave_next * forward_accel[moment].astype(jnp.float32)
        wave_prev, wave = wave, wave_next
    kernel = (-2.0 / velocity) * accumulated
    sensitivity = jnp.transpose(coarsen(kernel), (0, 2, 1))
    return sensitivity, wave
```

```python
import functools

import jax
import jax.numpy as jnp
from jax import lax
from jax.experimental import pallas as pl
from jax.experimental.pallas import tpu as pltpu
from jax.sharding import PartitionSpec as P

F32, BF16, I32 = jnp.float32, jnp.bfloat16, jnp.int32
NEAR = 3
VMEM = pl.BlockSpec(memory_space=pltpu.VMEM)


def iota(shape, dim):
    return lax.broadcasted_iota(I32, shape, dim)


def dot_t(a, b):
    return lax.dot_general(a, b, (((1,), (1,)), ((), ())), preferred_element_type=F32)


def parts_of(x, count):
    parts = []
    for _ in range(count):
        part = x.astype(BF16)
        parts.append(part)
        x = x - part.astype(F32)
    return parts


def one_hot(flags):
    return jnp.where(flags, 1.0, 0.0).astype(BF16)


def y_sides(n_gy):
    return ("swap",) if n_gy == 2 else ("high", "low")


def send_row(side, j, cy, reach):
    if side == "swap":
        return (cy - reach) * (1 - j)
    return 0 if side == "high" else cy - reach


def side_source(side, j, n_gy, cy, reach):
    if side == "swap":
        return 1 - j, (cy - reach) * j, j >= 0
    if side == "high":
        return jnp.minimum(j + 1, n_gy - 1), 0, j + 1 < n_gy
    return jnp.maximum(j - 1, 0), cy - reach, j > 0


def pack_kernel(n_gx, n_gy, steps, slots, panels_ref, owner_ref, cell_ref, offset_ref, out_ref):
    sensors, length = panels_ref.shape
    half = length // steps
    span = 2 * half
    row, sample = iota((span * steps, length), 0), iota((span * steps, length), 1)
    clock = (sample + row // steps).astype(F32)
    centre = ((row % steps + 1) * half).astype(F32)
    weights = jnp.maximum(0.0, 1.0 - jnp.abs(clock - centre) * (1.0 / half)) * 0.25
    shifted = dot_t(weights.astype(BF16), panels_ref[...])
    offsets = offset_ref[...]
    amplitudes = jnp.zeros((steps, sensors), F32)
    for o in range(span):
        amplitudes = jnp.where(offsets == o, shifted[o * steps : (o + 1) * steps], amplitudes)
    owners = owner_ref[...]
    named = iota((n_gx, sensors), 0) == owners
    earlier = one_hot(iota((sensors, sensors), 0) <= iota((sensors, sensors), 1))
    counts = jnp.dot(one_hot(named), earlier, preferred_element_type=F32)
    rank = jnp.sum(jnp.where(named, counts, 0.0), axis=0, keepdims=True).astype(I32) - 1
    target = owners * slots + rank
    places = n_gx * slots
    moved = one_hot(iota((places, sensors), 0) == target)
    code = cell_ref[...] + 1
    line = iota((8, sensors), 0)
    code_rows = jnp.where(line == 0, code >> 8, jnp.where(line == 1, code & 255, 0))
    rows = parts_of(amplitudes, 3) + [code_rows.astype(F32).astype(BF16)]
    packed = [dot_t(part, moved) for part in rows]
    packed_amp = packed[0] + packed[1] + packed[2]
    packed_code = packed[3][0:1] * 256.0 + packed[3][1:2]
    blank = jnp.zeros((8, 128), F32)
    width = places + 128
    amp_pad = pltpu.roll(jnp.concatenate([packed_amp, blank], axis=1), slots, 1)
    code_pad = jnp.concatenate([jnp.broadcast_to(packed_code, (8, places)), blank], axis=1)
    code_pad = pltpu.roll(code_pad, slots, 1)
    line = iota((8, width), 0)
    lines = jnp.zeros((8, width), F32)
    for r in range(3):
        lines = jnp.where(line == r, pltpu.roll(code_pad, (3 - r) * slots, 1), lines)
    lane = iota((8, 128), 1)
    for g in range(n_gx):
        at = (g * slots) // 128 * 128
        turn = (256 - (g * slots) % 128) % 256
        if at + 256 <= width:
            amp_window, code_window = amp_pad[:, at : at + 256], lines[:, at : at + 256]
            if turn:
                amp_window, code_window = pltpu.roll(amp_window, turn, 1), pltpu.roll(code_window, turn, 1)
        else:
            amp_window, code_window = amp_pad[:, at : at + 128], lines[:, at : at + 128]
        tile = jnp.where(lane < 3 * slots, amp_window[:, :128], code_window[:, :128])
        for j in range(n_gy):
            out_ref[g, j] = tile


def plane_counts(cx):
    return (cx, cx, cx - 1, cx - 1)


def prep_kernel(n_gy, reach, now_ref, rho_ref, last_ref, vel_ref, odd_ref, even_ref, *side_refs):
    cx, cy, nz = now_ref.shape
    i, j = lax.axis_index("gx"), lax.axis_index("gy")
    parity = lax.rem(i, 2)
    fields = (now_ref, rho_ref, last_ref, vel_ref)
    for out_ref, right in ((odd_ref, parity), (even_ref, 1 - parity)):
        at = 0
        for ref, count in zip(fields, plane_counts(cx)):
            first = right if count < cx else 0
            out_ref[at : at + count] = ref[pl.ds(first, count)].astype(BF16)
            at += count
        near = (cx - NEAR) * right
        for ref in fields:
            x = ref[pl.ds(near, NEAR)]
            out_ref[at : at + NEAR] = (x - x.astype(BF16).astype(F32)).astype(BF16)
            at += NEAR
    for n, side in enumerate(y_sides(n_gy)):
        row = send_row(side, j, cy, reach)
        y_ref, corner_ref = side_refs[2 * n], side_refs[2 * n + 1]
        for f, ref in enumerate(fields):
            x = ref[:, pl.ds(pl.multiple_of(row, reach), reach), :]
            y_ref[f] = x
            corner_ref[f] = x.reshape(cx * reach, nz).astype(BF16)


def sim_kernel(n_gx, n_gy, steps, slots, reach, *refs):
    sides = y_sides(n_gy)
    now_ref, rho_ref, last_ref, vel_ref, forward_ref, arrived_ref, odd_ref, even_ref = refs[:8]
    side_refs = refs[8 : 8 + 3 * len(sides)]
    outs = refs[8 + 3 * len(sides) :]
    if n_gy == 2:
        final_ref, mine_ref, send_ref = outs[:3]
        scratch = outs[3:]
    else:
        final_ref, coarse_ref = outs[:2]
        scratch = outs[2:]
    (w_ref, prev_ref, r_ref, s_ref, c0, cxu, cxd, cyu, cyd, czu, czd, inject, acc_ref, flat_ref) = scratch
    cx, cy, nz = now_ref.shape
    rows = cy + reach * len(sides)
    i, j = lax.axis_index("gx"), lax.axis_index("gy")
    parity = lax.rem(i, 2)

    ext = (w_ref, r_ref, prev_ref, s_ref)
    for ref, out in zip((now_ref, rho_ref, last_ref, vel_ref), ext):
        out[cx : 2 * cx, 0:cy] = ref[...]
    for ref, left in ((odd_ref, 1 - parity), (even_ref, parity)):
        base = 2 * cx * (1 - left)
        at = 0
        for out, count in zip(ext, plane_counts(cx)):
            first = base + left if count < cx else base
            out[pl.ds(first, count), 0:cy] = ref[at : at + count].astype(F32)
            at += count
        near = base + (cx - NEAR) * left
        for out in ext:
            out[pl.ds(near, NEAR), 0:cy] += ref[at : at + NEAR].astype(F32)
            at += NEAR
    for n in range(len(sides)):
        own_side, even_side, odd_side = side_refs[3 * n : 3 * n + 3]
        at = cy + reach * n
        for f, out in enumerate(ext):
            out[cx : 2 * cx, at : at + reach] = own_side[f]
            out[pl.ds(2 * cx * (1 - parity), cx), at : at + reach] = even_side[f]
            corner = odd_side[f].astype(F32).reshape(cx, reach, nz)
            out[pl.ds(2 * cx * parity, cx), at : at + reach] = corner

    width = slots * n_gx
    per = 128 // slots
    lane = iota((8, 128), 1)

    def gathered(strip, slab):
        tiles, codes = [], []
        for g0 in range(0, n_gx, per):
            tile, code = jnp.zeros((8, 128), F32), jnp.zeros((8, 128), F32)
            for k in range(per):
                x = arrived_ref[g0 + k, strip]
                here = (lane >= k * slots) & (lane < (k + 1) * slots)
                turn = ((k - slab) * slots) % 128
                tile = jnp.where(here, pltpu.roll(x, turn, 1) if turn else x, tile)
                turn = ((k - 3) * slots) % 128
                code = jnp.where(here, pltpu.roll(x, turn, 1) if turn else x, code)
            tiles.append(tile)
            codes.append(code[slab : slab + 1])
        return jnp.concatenate(tiles, axis=1), jnp.concatenate(codes, axis=1).astype(I32) - 1

    depths = iota((nz, width), 0)
    for slab in range(3):
        layers = [(max(t + 1 - cx * slab, 0), min(3 * cx - 1 - t - cx * slab, cx)) for t in range(steps)]
        amps, codes = gathered(j, slab)
        depth = one_hot(depths == (codes & (nz - 1)))
        cells = one_hot(iota((cx * cy, width), 0) == (codes >> 8))
        hi, lo = parts_of(amps, 2)
        for t in range(steps):
            a, b = layers[t]
            if b <= a:
                continue
            block = cells[a * cy : b * cy]
            out = dot_t(block * hi[t : t + 1], depth) + dot_t(block * lo[t : t + 1], depth)
            inject[t, slab * cx + a : slab * cx + b, 0:cy] = out.reshape(b - a, cy, nz)
        for n, side in enumerate(sides):
            strip, row, there = side_source(side, j, n_gy, cy, reach)
            amps, codes = gathered(strip, slab)
            depth = one_hot(depths == (codes & (nz - 1)))
            place = codes >> 8
            y = (place & (cy - 1)) - row
            inside = (codes >= 0) & (y >= 0) & (y < reach) & there
            place = jnp.where(inside, (place // cy) * reach + y, -1)
            cells = one_hot(iota((cx * reach, width), 0) == place)
            hi, lo = parts_of(amps, 2)
            block = jnp.concatenate([cells * hi[t : t + 1] for t in range(steps)], axis=0)
            out = dot_t(block, depth)
            block = jnp.concatenate([cells * lo[t : t + 1] for t in range(steps)], axis=0)
            out = (out + dot_t(block, depth)).reshape(steps, cx, reach, nz)
            at = cy + reach * n
            for t in range(steps):
                inject[t, slab * cx : (slab + 1) * cx, at : at + reach] = out[t]

    row_at, lane_at = iota((rows, nz), 0), iota((rows, nz), 1)
    brk = cy + reach - 1 if n_gy > 2 else jnp.where(j == 0, rows - 1, cy - 1)
    before = jnp.where(brk == rows - 1, 0, brk + 1)
    top, bottom = row_at == brk, row_at == before
    deep, shallow = lane_at == nz - 1, lane_at == 0

    def over(x):
        return 2.0 / jnp.where(x > 0.0, x, 1.0)

    def couple(x, carry):
        rho = r_ref[x]
        vel = 0.11 * s_ref[x]
        stiff = vel * vel * rho
        alone = over(rho)
        hxu, hxd = over(rho + r_ref[x + 1]), over(rho + r_ref[x - 1])
        hyu = jnp.where(top, alone, over(rho + pltpu.roll(rho, rows - 1, 0)))
        hyd = jnp.where(bottom, alone, pltpu.roll(hyu, 1, 0))
        hzu = jnp.where(deep, alone, over(rho + pltpu.roll(rho, nz - 1, 1)))
        hzd = jnp.where(shallow, alone, pltpu.roll(hzu, 1, 1))
        c0[x] = 2.0 - stiff * (((hxu + hxd) + (hyu + hyd)) + (hzu + hzd))
        cxu[x], cxd[x] = stiff * hxu, stiff * hxd
        cyu[x] = jnp.where(top, 0.0, stiff * hyu)
        cyd[x] = jnp.where(bottom, 0.0, stiff * hyd)
        czu[x] = jnp.where(deep, 0.0, stiff * hzu)
        czd[x] = jnp.where(shallow, 0.0, stiff * hzd)
        return carry

    lax.fori_loop(1, 3 * cx - 1, couple, 0)

    wave, prev = w_ref, prev_ref
    for t in range(steps):

        def stencil(x, wave=wave, prev=prev, t=t):
            w = wave[x]
            u = c0[x] * w - prev[x] + inject[t, x]
            u = u + (cxu[x] * wave[x + 1] + cxd[x] * wave[x - 1])
            u = u + (cyu[x] * pltpu.roll(w, rows - 1, 0) + cyd[x] * pltpu.roll(w, 1, 0))
            return u + (czu[x] * pltpu.roll(w, nz - 1, 1) + czd[x] * pltpu.roll(w, 1, 1))

        def outer(x, carry, prev=prev, stencil=stencil):
            prev[x] = stencil(x)
            return carry

        def inner(x, carry, prev=prev, stencil=stencil, t=t):
            u = stencil(x)
            term = u[0:cy] * forward_ref[t, x - cx].astype(F32)
            acc_ref[x - cx] = term if t == 0 else acc_ref[x - cx] + term
            if t == steps - 1:
                final_ref[x - cx] = u[0:cy]
            else:
                prev[x] = u
            return carry

        lax.fori_loop(t + 1, cx, outer, 0)
        lax.fori_loop(cx, 2 * cx, inner, 0)
        lax.fori_loop(2 * cx, 3 * cx - 1 - t, outer, 0)
        wave, prev = prev, wave

    blocks = []
    for a in range(0, cx, 2):
        pair = (-2.0 / vel_ref[a]) * acc_ref[a] + (-2.0 / vel_ref[a + 1]) * acc_ref[a + 1]
        blocks.append(pair * 0.125)
    flat = jnp.concatenate(blocks, axis=0)
    half_z = one_hot(iota((nz // 2, nz), 1) // 2 == iota((nz // 2, nz), 0))
    flat = sum(dot_t(half_z, part) for part in parts_of(flat, 3)[::-1])
    count = cx // 2 * cy
    at = iota((count, count if n_gy == 2 else count // 2), 0)
    to = iota((count, count if n_gy == 2 else count // 2), 1)
    if n_gy == 2:
        goal = at // cy * cy + j * (cy // 2) + at % cy // 2
    else:
        goal = at // 2
    half_y = one_hot(to == goal)
    flat = sum(jnp.dot(part, half_y, preferred_element_type=F32) for part in parts_of(flat, 3)[::-1])
    if n_gy == 2:
        flat_ref[...] = flat
        half = nz // 4
        mine_ref[...] = flat_ref[pl.ds(pl.multiple_of(j * half, half), half)]
        send_ref[...] = flat_ref[pl.ds(pl.multiple_of((1 - j) * half, half), half)]
    else:
        coarse_ref[...] = flat


def call(kernel, out_shape, args, scratch=(), limit=60 << 20):
    return pl.pallas_call(
        kernel,
        out_shape=out_shape,
        in_specs=[VMEM] * len(args),
        out_specs=jax.tree.map(lambda _: VMEM, out_shape),
        scratch_shapes=scratch,
        compiler_params=pltpu.CompilerParams(vmem_limit_bytes=limit),
    )(*args)


def shards(
    n_gx,
    n_gy,
    velocity,
    density,
    adjoint_last,
    adjoint_now,
    forward_accel,
    residual_panels,
    owner_slab,
    receiver_cell,
    trace_offset,
):
    cx, cy, nz = velocity.shape
    steps = forward_accel.shape[0]
    reach = steps
    sensors = residual_panels.shape[0]
    slots = sensors // 16
    sides = y_sides(n_gy)
    shape = jax.ShapeDtypeStruct
    fields = (adjoint_now, density, adjoint_last, velocity)

    planes = sum(plane_counts(cx)) + 4 * NEAR
    prep_out = [shape((planes, cy, nz), BF16)] * 2
    for _ in sides:
        prep_out += [shape((4, cx, reach, nz), F32), shape((4, cx * reach, nz), BF16)]
    prep = call(functools.partial(prep_kernel, n_gy, reach), prep_out, fields)
    odd = [(a, a + 1) for a in range(1, n_gx - 1, 2)]
    odd = odd + [(b, a) for a, b in odd]
    even = [(a, a ^ 1) for a in range(n_gx)]
    odd_got = lax.ppermute(prep[0], "gx", odd)
    side_got = []
    for n, side in enumerate(sides):
        if side == "swap":
            over_y = [(0, 1), (1, 0)]
        elif side == "high":
            over_y = [(b + 1, b) for b in range(n_gy - 1)]
        else:
            over_y = [(b, b + 1) for b in range(n_gy - 1)]
        corner = [(a * n_gy + c, b * n_gy + d) for a, b in odd for c, d in over_y]
        own_side = lax.ppermute(prep[2 + 2 * n], "gy", over_y)
        odd_side = lax.ppermute(prep[3 + 2 * n], ("gx", "gy"), corner)
        side_got.append((own_side, odd_side))
    even_got = lax.ppermute(prep[1], "gx", even)

    packed = call(
        functools.partial(pack_kernel, n_gx, n_gy, steps, slots),
        shape((n_gx, n_gy, 8, 128), F32),
        (
            residual_panels,
            owner_slab.reshape(1, sensors),
            receiver_cell.reshape(1, sensors),
            trace_offset.reshape(1, sensors),
        ),
    )
    arrived = lax.all_to_all(
        packed.reshape(n_gx * n_gy, 8, 128), ("gx", "gy"), split_axis=0, concat_axis=0, tiled=True
    ).reshape(n_gx, n_gy, 8, 128)
    side_args = []
    for own_side, odd_side in side_got:
        side_args += [own_side, lax.ppermute(own_side, "gx", even), odd_side]

    rows = cy + reach * len(sides)
    block = pltpu.VMEM((3 * cx, rows, nz), F32)
    if n_gy == 2:
        outs = [shape((nz // 4, cx // 2 * cy), F32)] * 2
    else:
        outs = [shape((nz // 2, cx * cy // 4), F32)]
    got = call(
        functools.partial(sim_kernel, n_gx, n_gy, steps, slots, reach),
        [shape((cx, cy, nz), F32)] + outs,
        fields + (forward_accel, arrived, odd_got, even_got) + tuple(side_args),
        [block] * 11
        + [
            pltpu.VMEM((steps, 3 * cx, rows, nz), F32),
            pltpu.VMEM((cx, cy, nz), F32),
            pltpu.VMEM((nz // 2, cx // 2 * cy), F32),
        ],
    )
    if n_gy == 2:
        final, mine, send = got
        whole = mine + lax.ppermute(send, "gy", [(0, 1), (1, 0)])
        sensitivity = jnp.transpose(whole.reshape(nz // 4, cx // 2, cy), (1, 0, 2))
    else:
        final, coarse = got
        coarse = jnp.transpose(coarse.reshape(nz // 2, cx // 2, cy // 2), (1, 0, 2))
        sensitivity = lax.all_to_all(coarse, "gy", split_axis=1, concat_axis=2, tiled=True)
    return sensitivity, final


def solution(mesh):
    in_specs = (
        P("gx", "gy", None),
        P("gx", "gy", None),
        P("gx", "gy", None),
        P("gx", "gy", None),
        P(None, "gx", "gy", None),
        P(("gx", "gy"), None),
        P(("gx", "gy"), None),
        P(("gx", "gy")),
        P(("gx", "gy")),
    )
    out_specs = (P("gx", "gy", None), P("gx", "gy", None))
    body = functools.partial(shards, mesh.shape["gx"], mesh.shape["gy"])
    return jax.shard_map(body, mesh=mesh, in_specs=in_specs, out_specs=out_specs, check_vma=False)
```

```python
import functools

import jax
import jax.numpy as jnp
from jax import lax
from jax.experimental import pallas as pl
from jax.experimental.pallas import tpu as pltpu
from jax.sharding import PartitionSpec as P

F32, BF16, I32 = jnp.float32, jnp.bfloat16, jnp.int32
NEAR = 3
NEAR_CORNER = 4
VMEM = pl.BlockSpec(memory_space=pltpu.VMEM)
ANY = pl.BlockSpec(memory_space=pl.ANY)
HBM = pl.BlockSpec(memory_space=pltpu.HBM)


def iota(shape, dim):
    return lax.broadcasted_iota(I32, shape, dim)


def dot_t(a, b):
    return lax.dot_general(a, b, (((1,), (1,)), ((), ())), preferred_element_type=F32)


def parts_of(x, count):
    parts = []
    for _ in range(count):
        part = x.astype(BF16)
        parts.append(part)
        x = x - part.astype(F32)
    return parts


def one_hot(flags):
    return jnp.where(flags, 1.0, 0.0).astype(BF16)


def y_sides(n_gy):
    return ("swap",) if n_gy == 2 else ("high", "low")


def send_row(side, j, cy, reach):
    if side == "swap":
        return (cy - reach) * (1 - j)
    return 0 if side == "high" else cy - reach


def side_source(side, j, n_gy, cy, reach):
    if side == "swap":
        return 1 - j, (cy - reach) * j, j >= 0
    if side == "high":
        return jnp.minimum(j + 1, n_gy - 1), 0, j + 1 < n_gy
    return jnp.maximum(j - 1, 0), cy - reach, j > 0


def pack_kernel(n_gx, n_gy, steps, slots, panels_ref, owner_ref, cell_ref, offset_ref, out_ref):
    sensors, length = panels_ref.shape
    half = length // steps
    span = 2 * half
    row, sample = iota((span * steps, length), 0), iota((span * steps, length), 1)
    clock = (sample + row // steps).astype(F32)
    centre = ((row % steps + 1) * half).astype(F32)
    weights = jnp.maximum(0.0, 1.0 - jnp.abs(clock - centre) * (1.0 / half)) * 0.25
    shifted = dot_t(weights.astype(BF16), panels_ref[...])
    offsets = offset_ref[...]
    amplitudes = jnp.zeros((steps, sensors), F32)
    for o in range(span):
        amplitudes = jnp.where(offsets == o, shifted[o * steps : (o + 1) * steps], amplitudes)
    owners = owner_ref[...]
    named = iota((n_gx, sensors), 0) == owners
    earlier = one_hot(iota((sensors, sensors), 0) <= iota((sensors, sensors), 1))
    counts = jnp.dot(one_hot(named), earlier, preferred_element_type=F32)
    rank = jnp.sum(jnp.where(named, counts, 0.0), axis=0, keepdims=True).astype(I32) - 1
    target = owners * slots + rank
    places = n_gx * slots
    moved = one_hot(iota((places, sensors), 0) == target)
    code = cell_ref[...] + 1
    line = iota((8, sensors), 0)
    code_rows = jnp.where(line == 0, code >> 8, jnp.where(line == 1, code & 255, 0))
    rows = parts_of(amplitudes, 3) + [code_rows.astype(F32).astype(BF16)]
    packed = [dot_t(part, moved) for part in rows]
    packed_amp = packed[0] + packed[1] + packed[2]
    packed_code = packed[3][0:1] * 256.0 + packed[3][1:2]
    blank = jnp.zeros((8, 128), F32)
    width = places + 128
    amp_pad = pltpu.roll(jnp.concatenate([packed_amp, blank], axis=1), slots, 1)
    code_pad = jnp.concatenate([jnp.broadcast_to(packed_code, (8, places)), blank], axis=1)
    code_pad = pltpu.roll(code_pad, slots, 1)
    line = iota((8, width), 0)
    lines = jnp.zeros((8, width), F32)
    for r in range(3):
        lines = jnp.where(line == r, pltpu.roll(code_pad, (3 - r) * slots, 1), lines)
    lane = iota((8, 128), 1)
    for g in range(n_gx):
        at = (g * slots) // 128 * 128
        turn = (256 - (g * slots) % 128) % 256
        if at + 256 <= width:
            amp_window, code_window = amp_pad[:, at : at + 256], lines[:, at : at + 256]
            if turn:
                amp_window, code_window = pltpu.roll(amp_window, turn, 1), pltpu.roll(code_window, turn, 1)
        else:
            amp_window, code_window = amp_pad[:, at : at + 128], lines[:, at : at + 128]
        tile = jnp.where(lane < 3 * slots, amp_window[:, :128], code_window[:, :128])
        for j in range(n_gy):
            out_ref[g, j] = tile


def plane_counts(cx):
    return (cx, cx, cx - 1, cx - 1)


def prep_kernel(n_gy, reach, now_ref, rho_ref, last_ref, vel_ref, odd_ref, even_ref, *side_refs):
    cx, cy, nz = now_ref.shape
    i, j = lax.axis_index("gx"), lax.axis_index("gy")
    parity = lax.rem(i, 2)
    fields = (now_ref, rho_ref, last_ref, vel_ref)
    for out_ref, right in ((odd_ref, parity), (even_ref, 1 - parity)):
        at = 0
        for ref, count in zip(fields, plane_counts(cx)):
            first = right if count < cx else 0
            out_ref[at : at + count] = ref[pl.ds(first, count)].astype(BF16)
            at += count
        near = (cx - NEAR) * right
        for ref in fields:
            x = ref[pl.ds(near, NEAR)]
            out_ref[at : at + NEAR] = (x - x.astype(BF16).astype(F32)).astype(BF16)
            at += NEAR
    for n, side in enumerate(y_sides(n_gy)):
        row = send_row(side, j, cy, reach)
        y_ref, corner_ref = side_refs[3 * n], side_refs[3 * n + 1]
        for f, ref in enumerate(fields):
            x = ref[:, pl.ds(pl.multiple_of(row, reach), reach), :]
            y_ref[f] = x
            for out_ref, right in ((corner_ref, parity), (side_refs[3 * n + 2], 1 - parity)):
                out_ref[f, 0 : cx * reach] = x.reshape(cx * reach, nz).astype(BF16)
                z = ref[pl.ds((cx - NEAR_CORNER) * right, NEAR_CORNER), pl.ds(pl.multiple_of(row, reach), reach), :]
                z = (z - z.astype(BF16).astype(F32)).reshape(NEAR_CORNER * reach, nz)
                out_ref[f, cx * reach :] = z.astype(BF16)


def sim_kernel(n_gx, n_gy, steps, slots, reach, *refs):
    sides = y_sides(n_gy)
    fields, forward_in, arrived_in, odd_in, even_in = refs[:4], *refs[4:8]
    side_in = refs[8 : 8 + 3 * len(sides)]
    refs = refs[8 + 3 * len(sides) :]
    final_out = refs[0]
    coarse_refs, refs = (refs[1:3], refs[3:]) if n_gy == 2 else (refs[1:2], refs[2:])
    (w_ref, r_ref, prev_ref, v_ref, c0, cxu, cxd, cyu, cyd, czu, czd, inject, acc_ref), refs = refs[:13], refs[13:]
    forward_ref, arrived_ref, odd_ref, even_ref, *corner_refs, sem = refs
    cx, cy, nz = fields[0].shape
    half = nz // 2
    halves = range(2)
    rows = cy + reach * len(sides)
    pad = 8
    i, j = lax.axis_index("gx"), lax.axis_index("gy")
    parity = lax.rem(i, 2)
    if n_gy == 2:
        own, halo = pad + reach * j, (pad + cy * (1 - j),)
    else:
        own, halo = pad + reach, (pad + reach + cy, pad)
    own = pl.multiple_of(own, 8)
    halo = [pl.multiple_of(at, 8) for at in halo]
    own_rows = pl.ds(own, cy)
    ext = (w_ref, r_ref, prev_ref, v_ref)
    even_base, odd_base = 2 * cx * (1 - parity), 2 * cx * parity

    copies = []

    def fetch(src, dst):
        copy = pltpu.make_async_copy(src, dst, sem.at[len(copies)])
        copy.start()
        copies.append(copy)
        return copy

    got_sensors = fetch(arrived_in, arrived_ref)
    got_fields = []
    for field, out in zip(fields, ext):
        for h in halves:
            got_fields.append(fetch(field.at[:, :, half * h : half * (h + 1)], out.at[cx : 2 * cx, h, own_rows]))
    got_halos = [fetch(odd_in, odd_ref), fetch(even_in, even_ref)]
    for n in range(len(sides)):
        own_side, even_side, odd_side = side_in[3 * n : 3 * n + 3]
        for f, out in enumerate(ext):
            for h in halves:
                lanes = slice(half * h, half * (h + 1))
                at = pl.ds(halo[n], reach)
                got_fields.append(fetch(own_side.at[f, :, :, lanes], out.at[cx : 2 * cx, h, at]))
        got_halos.append(fetch(odd_side, corner_refs[2 * n]))
        got_halos.append(fetch(even_side, corner_refs[2 * n + 1]))
    got_forward = fetch(forward_in, forward_ref)

    blank = jnp.zeros((3 * cx, 2, pad, half), F32)
    for out in (w_ref, r_ref, prev_ref):
        out[:, :, 0:pad] = blank
        out[:, :, pad + rows : pad + rows + 8] = blank

    width = slots * n_gx
    per = 128 // slots
    lane = iota((8, 128), 1)

    def turned(x, turn):
        return pltpu.roll(x, turn % 128, 1) if turn % 128 else x

    def gathered(strip):
        tiles, codes = [[], [], []], []
        for g0 in range(0, n_gx, per):
            tile, code = [jnp.zeros((8, 128), F32)] * 3, jnp.zeros((8, 128), F32)
            for k in range(per):
                x = arrived_ref[g0 + k, strip]
                here = (lane >= k * slots) & (lane < (k + 1) * slots)
                for slab in range(3):
                    tile[slab] = jnp.where(here, turned(x, (k - slab) * slots), tile[slab])
                code = jnp.where(here, turned(x, (k - 3) * slots), code)
            for slab in range(3):
                tiles[slab].append(tile[slab])
            codes.append(code)
        codes = jnp.concatenate(codes, axis=1)
        return [jnp.concatenate(t, axis=1) for t in tiles], codes.astype(I32) - 1, jnp.transpose(codes).astype(I32) - 1

    def spread(cells_at, amps, column, spans):
        depth = one_hot(iota((width, nz), 1) == (column & (nz - 1)))
        hi, lo = parts_of(amps, 2)
        out = 0.0
        for part in (lo, hi):
            block = jnp.concatenate([cells_at[a:b] * part[t : t + 1] for t, a, b in spans], axis=0)
            out = out + jnp.dot(block, depth, preferred_element_type=F32)
        return out

    got_sensors.wait()
    strips = [(j, None)]
    for side in sides:
        strip, row, there = side_source(side, j, n_gy, cy, reach)
        strips.append((strip, (row, there)))
    for n, (strip, beside) in enumerate(strips):
        amps, codes, columns = gathered(strip)
        tall = cy if beside is None else reach
        at = pl.ds(own - pad if beside is None else halo[n - 1] - pad, tall)
        for slab in range(3):
            code = codes[slab : slab + 1]
            place = code >> 8
            if beside is not None:
                y = (place & (cy - 1)) - beside[0]
                inside = (code >= 0) & (y >= 0) & (y < reach) & beside[1]
                place = jnp.where(inside, (place // cy) * reach + y, -1)
            cells = one_hot(iota((cx * tall, width), 0) == place)
            layers = [(max(t + 1 - cx * slab, 0), min(3 * cx - 1 - t - cx * slab, cx)) for t in range(steps)]
            spans = [(t, a * tall, b * tall) for t, (a, b) in enumerate(layers) if a < b]
            out = spread(cells, amps[slab], columns[:, slab : slab + 1], spans)
            first = 0
            for t, a, b in spans:
                value = out[first : first + b - a].reshape((b - a) // tall, tall, nz)
                first += b - a
                xs = slice(slab * cx + a // tall, slab * cx + b // tall)
                for h in halves:
                    inject[t, xs, h, at] = value[:, :, half * h : half * (h + 1)]

    for copy in got_fields + got_halos:
        copy.wait()
    for ref, left in ((odd_ref, 1 - parity), (even_ref, parity)):
        base = 2 * cx * (1 - left)
        at = 0
        for out, count in zip(ext, plane_counts(cx)):
            first = base + left if count < cx else base
            for h in halves:
                lanes = slice(half * h, half * (h + 1))
                out[pl.ds(first, count), h, own_rows] = ref[at : at + count, :, lanes].astype(F32)
            at += count
        near = base + (cx - NEAR) * left
        for out in ext:
            for h in halves:
                lanes = slice(half * h, half * (h + 1))
                out[pl.ds(near, NEAR), h, own_rows] += ref[at : at + NEAR, :, lanes].astype(F32)
            at += NEAR
    for n in range(len(sides)):
        for f, out in enumerate(ext):
            for ref, left in ((corner_refs[2 * n], 1 - parity), (corner_refs[2 * n + 1], parity)):
                corner = ref[f].astype(F32).reshape(cx + NEAR_CORNER, reach, nz)
                base = 2 * cx * (1 - left)
                near = base + (cx - NEAR_CORNER) * left
                for h in halves:
                    lanes, at = slice(half * h, half * (h + 1)), pl.ds(halo[n], reach)
                    out[pl.ds(base, cx), h, at] = corner[:cx, :, lanes]
                    out[pl.ds(near, NEAR_CORNER), h, at] += corner[cx:, :, lanes]

    lane = iota((rows, half), 1)
    last, first = lane == half - 1, lane == 0
    mid, above, below = slice(pad, pad + rows), slice(pad + 1, pad + rows + 1), slice(pad - 1, pad + rows - 1)

    def shifted(x0, x1):
        u0, u1 = pltpu.roll(x0, half - 1, 1), pltpu.roll(x1, half - 1, 1)
        d0, d1 = pltpu.roll(x0, 1, 1), pltpu.roll(x1, 1, 1)
        return (jnp.where(last, u1, u0), u1), (d0, jnp.where(first, d0, d1))

    def over(x):
        return 2.0 / jnp.maximum(x, 1.0)

    def couple(x):
        rho = [r_ref[x, h, mid] for h in halves]
        deep, shallow = shifted(*rho)
        deep = (deep[0], jnp.where(last, 0.0, deep[1]))
        shallow = (jnp.where(first, 0.0, shallow[0]), shallow[1])
        for h in halves:
            vel = 0.11 * v_ref[x, h, mid]
            stiff = vel * vel * rho[h]
            xu, xd = stiff * over(rho[h] + r_ref[x + 1, h, mid]), stiff * over(rho[h] + r_ref[x - 1, h, mid])
            yu, yd = stiff * over(rho[h] + r_ref[x, h, above]), stiff * over(rho[h] + r_ref[x, h, below])
            zu, zd = stiff * over(rho[h] + deep[h]), stiff * over(rho[h] + shallow[h])
            c0[x, h] = 2.0 - (((xu + xd) + (yu + yd)) + (zu + zd))
            cxu[x, h], cxd[x, h], cyu[x, h], cyd[x, h] = xu, xd, yu, yd
            czu[x, h] = jnp.where(last, 0.0, zu) if h == 1 else zu
            czd[x, h] = jnp.where(first, 0.0, zd) if h == 0 else zd

    for x in range(1, 3 * cx - 1):
        couple(x)
    got_forward.wait()

    wave, prev = w_ref, prev_ref
    for t in range(steps):

        def advance(x, wave=wave, prev=prev, t=t):
            w = [wave[x, h, mid] for h in halves]
            deep, shallow = shifted(*w)
            for h in halves:
                u = c0[x, h] * w[h] - prev[x, h, mid] + inject[t, x, h]
                u = u + (cxu[x, h] * wave[x + 1, h, mid] + cxd[x, h] * wave[x - 1, h, mid])
                u = u + (cyu[x, h] * wave[x, h, above] + cyd[x, h] * wave[x, h, below])
                prev[x, h, mid] = u + (czu[x, h] * deep[h] + czd[x, h] * shallow[h])

        def gather(x, prev=prev, t=t):
            for h in halves:
                term = prev[cx + x, h, own_rows] * forward_ref[t, x, :, half * h : half * (h + 1)].astype(F32)
                acc_ref[x, h] = term if t == 0 else acc_ref[x, h] + term

        for x in range(t + 1, 3 * cx - 1 - t):
            advance(x)
            if cx <= x < 2 * cx:
                gather(x - cx)
        wave, prev = prev, wave
    out_copies = [
        fetch(wave.at[cx : 2 * cx, h, own_rows], final_out.at[:, :, half * h : half * (h + 1)]) for h in halves
    ]

    flat = []
    for h in halves:
        blocks = []
        for a in range(0, cx, 2):
            pair = sum((-0.25 / v_ref[cx + b, h, own_rows]) * acc_ref[b, h] for b in (a, a + 1))
            blocks.append(pair)
        flat.append(jnp.concatenate(blocks, axis=0))
    if n_gy == 2:
        flat = [jnp.where(j == h, flat[0], flat[1]) for h in halves]
    half_z = one_hot(iota((half, half // 2), 0) // 2 == iota((half, half // 2), 1))
    count = cx // 2 * cy
    tall = count if n_gy == 2 else count // 2
    to, at = iota((tall, count), 0), iota((tall, count), 1)
    goal = at // cy * cy + j * (cy // 2) + at % cy // 2 if n_gy == 2 else at // 2
    half_y = one_hot(to == goal)
    for h in halves:
        x = sum(jnp.dot(part, half_z, preferred_element_type=F32) for part in parts_of(flat[h], 3)[::-1])
        x = sum(jnp.dot(half_y, part, preferred_element_type=F32) for part in parts_of(x, 3)[::-1])
        if n_gy == 2:
            coarse_refs[h][...] = x.reshape(cx // 2, cy, half // 2)
        else:
            coarse_refs[0][:, half // 2 * h : half // 2 * (h + 1)] = x
    for copy in out_copies:
        copy.wait()


def call(kernel, out_shape, args, scratch=(), in_specs=None, out_specs=None, limit=60 << 20):
    return pl.pallas_call(
        kernel,
        out_shape=out_shape,
        in_specs=in_specs or [VMEM] * len(args),
        out_specs=out_specs or jax.tree.map(lambda _: VMEM, out_shape),
        scratch_shapes=scratch,
        compiler_params=pltpu.CompilerParams(vmem_limit_bytes=limit),
    )(*args)


def shards(
    n_gx,
    n_gy,
    velocity,
    density,
    adjoint_last,
    adjoint_now,
    forward_accel,
    residual_panels,
    owner_slab,
    receiver_cell,
    trace_offset,
):
    cx, cy, nz = velocity.shape
    steps = forward_accel.shape[0]
    reach = steps
    sensors = residual_panels.shape[0]
    slots = sensors // 16
    sides = y_sides(n_gy)
    shape = jax.ShapeDtypeStruct
    fields = (adjoint_now, density, adjoint_last, velocity)

    planes = sum(plane_counts(cx)) + 4 * NEAR
    prep_out = [shape((planes, cy, nz), BF16)] * 2
    for _ in sides:
        prep_out += [shape((4, cx, reach, nz), F32)] + [shape((4, (cx + NEAR_CORNER) * reach, nz), BF16)] * 2
    prep = call(functools.partial(prep_kernel, n_gy, reach), prep_out, fields)
    odd = [(a, a + 1) for a in range(1, n_gx - 1, 2)]
    odd = odd + [(b, a) for a, b in odd]
    even = [(a, a ^ 1) for a in range(n_gx)]
    packed = call(
        functools.partial(pack_kernel, n_gx, n_gy, steps, slots),
        shape((n_gx, n_gy, 8, 128), F32),
        (
            residual_panels,
            owner_slab.reshape(1, sensors),
            receiver_cell.reshape(1, sensors),
            trace_offset.reshape(1, sensors),
        ),
    )
    odd_got = lax.ppermute(prep[0], "gx", odd)
    side_got = []
    for n, side in enumerate(sides):
        if side == "swap":
            over_y = [(0, 1), (1, 0)]
        elif side == "high":
            over_y = [(b + 1, b) for b in range(n_gy - 1)]
        else:
            over_y = [(b, b + 1) for b in range(n_gy - 1)]
        corner = [(a * n_gy + c, b * n_gy + d) for a, b in odd for c, d in over_y]
        own_side = lax.ppermute(prep[2 + 3 * n], "gy", over_y)
        odd_side = lax.ppermute(prep[3 + 3 * n], ("gx", "gy"), corner)
        corner = [(a * n_gy + c, b * n_gy + d) for a, b in even for c, d in over_y]
        even_side = lax.ppermute(prep[4 + 3 * n], ("gx", "gy"), corner)
        side_got.append((own_side, even_side, odd_side))
    even_got = lax.ppermute(prep[1], "gx", even)

    arrived = lax.all_to_all(
        packed.reshape(n_gx * n_gy, 8, 128), ("gx", "gy"), split_axis=0, concat_axis=0, tiled=True
    ).reshape(n_gx, n_gy, 8, 128)
    side_args = [x for got in side_got for x in got]

    rows = cy + reach * len(sides)
    padded = pltpu.VMEM((3 * cx, 2, rows + 16, nz // 2), F32)
    block = pltpu.VMEM((3 * cx, 2, rows, nz // 2), F32)
    if n_gy == 2:
        outs = [shape((cx // 2, cy, nz // 4), F32)] * 2
    else:
        outs = [shape((cx * cy // 4, nz // 2), F32)]
    buffers = [forward_accel, arrived, odd_got, even_got] + [x for got in side_got for x in (got[2], got[1])]
    got = call(
        functools.partial(sim_kernel, n_gx, n_gy, steps, slots, reach),
        [shape((cx, cy, nz), F32)] + outs,
        fields + (forward_accel, arrived, odd_got, even_got) + tuple(side_args),
        [padded] * 4
        + [block] * 7
        + [pltpu.VMEM((steps, 3 * cx, 2, rows, nz // 2), F32), pltpu.VMEM((cx, 2, cy, nz // 2), F32)]
        + [pltpu.VMEM(x.shape, x.dtype) for x in buffers]
        + [pltpu.SemaphoreType.DMA((64,))],
        in_specs=[HBM] * 5 + [ANY] * (3 + len(side_args)),
        out_specs=[HBM] + [VMEM] * len(outs),
        limit=36 << 20,
    )
    if n_gy == 2:
        final, mine, send = got
        whole = mine + lax.ppermute(send, "gy", [(0, 1), (1, 0)])
        sensitivity = jnp.transpose(whole, (0, 2, 1))
    else:
        final, coarse = got
        coarse = jnp.transpose(coarse.reshape(cx // 2, cy // 2, nz // 2), (0, 2, 1))
        sensitivity = lax.all_to_all(coarse, "gy", split_axis=1, concat_axis=2, tiled=True)
    return sensitivity, final


def solution(mesh):
    in_specs = (
        P("gx", "gy", None),
        P("gx", "gy", None),
        P("gx", "gy", None),
        P("gx", "gy", None),
        P(None, "gx", "gy", None),
        P(("gx", "gy"), None),
        P(("gx", "gy"), None),
        P(("gx", "gy")),
        P(("gx", "gy")),
    )
    out_specs = (P("gx", "gy", None), P("gx", "gy", None))
    body = functools.partial(shards, mesh.shape["gx"], mesh.shape["gy"])
    return jax.shard_map(body, mesh=mesh, in_specs=in_specs, out_specs=out_specs, check_vma=False)
```

```python
import functools

import jax
import jax.numpy as jnp
from jax import lax
from jax.experimental import pallas as pl
from jax.experimental.pallas import tpu as pltpu
from jax.sharding import PartitionSpec as P

F32, BF16, I32 = jnp.float32, jnp.bfloat16, jnp.int32
NEAR = 3
NEAR_CORNER = 2
HALF_ROWS = 4
VMEM = pl.BlockSpec(memory_space=pltpu.VMEM)
ANY = pl.BlockSpec(memory_space=pl.ANY)
HBM = pl.BlockSpec(memory_space=pltpu.HBM)


def iota(shape, dim):
    return lax.broadcasted_iota(I32, shape, dim)


def dot_t(a, b):
    return lax.dot_general(a, b, (((1,), (1,)), ((), ())), preferred_element_type=F32)


def parts_of(x, count):
    parts = []
    for _ in range(count):
        part = x.astype(BF16)
        parts.append(part)
        x = x - part.astype(F32)
    return parts


def one_hot(flags):
    return jnp.where(flags, 1.0, 0.0).astype(BF16)


def y_sides(n_gy):
    return ("swap",) if n_gy == 2 else ("high", "low")


def send_row(side, j, cy, reach):
    if side == "swap":
        return (cy - reach) * (1 - j)
    return 0 if side == "high" else cy - reach


def side_source(side, j, n_gy, cy, reach):
    if side == "swap":
        return 1 - j, (cy - reach) * j, j >= 0
    if side == "high":
        return jnp.minimum(j + 1, n_gy - 1), 0, j + 1 < n_gy
    return jnp.maximum(j - 1, 0), cy - reach, j > 0


def pack_kernel(n_gx, n_gy, steps, slots, panels_ref, owner_ref, cell_ref, offset_ref, out_ref):
    sensors, length = panels_ref.shape
    half = length // steps
    span = 2 * half
    row, sample = iota((span * steps, length), 0), iota((span * steps, length), 1)
    clock = (sample + row // steps).astype(F32)
    centre = ((row % steps + 1) * half).astype(F32)
    weights = jnp.maximum(0.0, 1.0 - jnp.abs(clock - centre) * (1.0 / half)) * 0.25
    shifted = dot_t(weights.astype(BF16), panels_ref[...])
    offsets = offset_ref[...]
    amplitudes = jnp.zeros((steps, sensors), F32)
    for o in range(span):
        amplitudes = jnp.where(offsets == o, shifted[o * steps : (o + 1) * steps], amplitudes)
    owners = owner_ref[...]
    named = iota((n_gx, sensors), 0) == owners
    earlier = one_hot(iota((sensors, sensors), 0) <= iota((sensors, sensors), 1))
    counts = jnp.dot(one_hot(named), earlier, preferred_element_type=F32)
    rank = jnp.sum(jnp.where(named, counts, 0.0), axis=0, keepdims=True).astype(I32) - 1
    target = owners * slots + rank
    places = n_gx * slots
    moved = one_hot(iota((places, sensors), 0) == target)
    code = cell_ref[...] + 1
    line = iota((8, sensors), 0)
    code_rows = jnp.where(line == 0, code >> 8, jnp.where(line == 1, code & 255, 0))
    rows = parts_of(amplitudes, 3) + [code_rows.astype(F32).astype(BF16)]
    packed = [dot_t(part, moved) for part in rows]
    packed_amp = packed[0] + packed[1] + packed[2]
    packed_code = packed[3][0:1] * 256.0 + packed[3][1:2]
    blank = jnp.zeros((8, 128), F32)
    width = places + 128
    amp_pad = pltpu.roll(jnp.concatenate([packed_amp, blank], axis=1), slots, 1)
    code_pad = jnp.concatenate([jnp.broadcast_to(packed_code, (8, places)), blank], axis=1)
    code_pad = pltpu.roll(code_pad, slots, 1)
    line = iota((8, width), 0)
    lines = jnp.zeros((8, width), F32)
    for r in range(3):
        lines = jnp.where(line == r, pltpu.roll(code_pad, (3 - r) * slots, 1), lines)
    lane = iota((8, 128), 1)
    for g in range(n_gx):
        at = (g * slots) // 128 * 128
        turn = (256 - (g * slots) % 128) % 256
        if at + 256 <= width:
            amp_window, code_window = amp_pad[:, at : at + 256], lines[:, at : at + 256]
            if turn:
                amp_window, code_window = pltpu.roll(amp_window, turn, 1), pltpu.roll(code_window, turn, 1)
        else:
            amp_window, code_window = amp_pad[:, at : at + 128], lines[:, at : at + 128]
        tile = jnp.where(lane < 3 * slots, amp_window[:, :128], code_window[:, :128])
        for j in range(n_gy):
            out_ref[g, j] = tile


def plane_counts(cx):
    return (cx, cx, cx - 1, cx - 1)


def halo_planes(x_ref, out_ref, at, count, right):
    cx = x_ref.shape[0]
    first = right if count < cx else 0
    out_ref[at : at + count] = x_ref[pl.ds(first, count)].astype(BF16)
    x = x_ref[pl.ds((cx - NEAR) * right, NEAR)]
    out_ref[at + count : at + count + NEAR] = (x - x.astype(BF16).astype(F32)).astype(BF16)


def odd_kernel(*refs):
    given, out, held, made, sem = refs[:4], refs[4], refs[5:9], refs[9], refs[10]
    parity = lax.rem(lax.axis_index("gx"), 2)
    copies = [pltpu.make_async_copy(src, dst, sem.at[n]) for n, (src, dst) in enumerate(zip(given, held))]
    for copy in copies:
        copy.start()
    at, sent = 0, []
    for n, count in enumerate(plane_counts(held[0].shape[0])):
        copies[n].wait()
        halo_planes(held[n], made, at, count, parity)
        planes = pl.ds(at, count + NEAR)
        sent.append(pltpu.make_async_copy(made.at[planes], out.at[planes], sem.at[4 + n]))
        sent[-1].start()
        at += count + NEAR
    for copy in sent:
        copy.wait()


def second(x):
    return x - x.astype(BF16).astype(F32)


def fold(x, upper):
    up = jnp.where(upper, 1, 0)
    x = [x[n] for n in range(x.shape[0])]
    turned = [pltpu.roll(y, HALF_ROWS, 0) for y in x]
    row = iota(x[0].shape, 0)
    pairs = []
    for n in range(0, len(x), 2):
        later = jnp.where(up == 1, x[n], turned[n])
        sooner = jnp.where(up == 1, turned[n + 1], x[n + 1])
        pairs.append(jnp.where(row < HALF_ROWS, sooner, later))
    return pairs


def unfold(pairs, upper):
    up = jnp.where(upper, 1, 0)
    layers = []
    for y in pairs:
        turned = pltpu.roll(y, HALF_ROWS, 0)
        layers += [jnp.where(up == 1, y, turned), jnp.where(up == 1, turned, y)]
    return layers


def corner_tiles(cx):
    return cx // 2 + (cx // 2 + NEAR_CORNER) // 2


def tiles_of(x):
    return [x[n : n + 8] for n in range(0, x.shape[0], 8)]


def side_kernel(n_gy, reach, now_ref, rho_ref, last_ref, vel_ref, even_ref, *side_refs, done):
    cx, cy, nz = now_ref.shape
    i, j = lax.axis_index("gx"), lax.axis_index("gy")
    parity = lax.rem(i, 2)
    fields = (now_ref, rho_ref, last_ref, vel_ref)
    for n, side in enumerate(y_sides(n_gy)):
        row = send_row(side, j, cy, reach)
        rows = pl.ds(pl.multiple_of(row, reach), reach)
        y_ref, odd_ref, even_corner_ref = side_refs[3 * n : 3 * n + 3]
        upper = row > 0
        blocks = [[], []]
        mid = cx // 2
        for f, ref in enumerate(fields):
            y_ref[f] = ref[:, rows, :]
            for block, right in ((blocks[0], parity), (blocks[1], 1 - parity)):
                near = ref[pl.ds(mid * right, mid), rows, :]
                block += [near[m] for m in range(mid)]
                block += fold(ref[pl.ds(mid * (1 - right), mid), rows, :], upper)
                block += fold(second(ref[pl.ds((cx - NEAR_CORNER) * right, NEAR_CORNER), rows, :]), upper)
        for out_ref, block in zip((odd_ref, even_corner_ref), blocks):
            out_ref[...] = jnp.concatenate(block, axis=0).astype(BF16)
        for m in range(3):
            done(1 + 3 * n + m)
    at = 0
    for ref, count in zip(fields, plane_counts(cx)):
        halo_planes(ref, even_ref, at, count, 1 - parity)
        at += count + NEAR
    done(0)


def stage_kernel(n_gx, n_gy, steps, slots, reach, *refs):
    given, refs = refs[:8], refs[8:]
    count = 2 + 3 * len(y_sides(n_gy))
    outs, refs = refs[:count], refs[count:]
    held, made, sem = refs[:8], refs[8 : 8 + count], refs[8 + count]
    copies_in = [pltpu.make_async_copy(src, dst, sem.at[n]) for n, (src, dst) in enumerate(zip(given, held))]
    copies_out = [pltpu.make_async_copy(src, dst, sem.at[8 + n]) for n, (src, dst) in enumerate(zip(made, outs))]
    for copy in copies_in:
        copy.start()
    for copy in copies_in[:4]:
        copy.wait()
    pack_kernel(n_gx, n_gy, steps, slots, *held[:4], made[0])
    copies_out[0].start()
    for copy in copies_in[4:]:
        copy.wait()
    side_kernel(n_gy, reach, *held[4:], *made[1:], done=lambda n: copies_out[1 + n].start())
    for copy in copies_out:
        copy.wait()


def sim_kernel(n_gx, n_gy, steps, slots, reach, *refs):
    sides = y_sides(n_gy)
    fields, forward_in, arrived_in, odd_in, even_in = refs[:4], *refs[4:8]
    side_in = refs[8 : 8 + 3 * len(sides)]
    refs = refs[8 + 3 * len(sides) :]
    final_out = refs[0]
    coarse_refs, refs = (refs[1:3], refs[3:]) if n_gy == 2 else (refs[1:2], refs[2:])
    (w_ref, r_ref, prev_ref, v_ref, c0, cxu, cxd, cyu, cyd, czu, czd, inject, acc_ref), refs = refs[:13], refs[13:]
    forward_ref, arrived_ref, odd_ref, even_ref, *side_refs, sem = refs
    cx, cy, nz = fields[0].shape
    half = nz // 2
    halves = range(2)
    rows = cy + reach * len(sides)
    pad = 8
    i, j = lax.axis_index("gx"), lax.axis_index("gy")
    parity = lax.rem(i, 2)
    if n_gy == 2:
        own, halo = pad + reach * j, (pad + cy * (1 - j),)
    else:
        own, halo = pad + reach, (pad + reach + cy, pad)
    own = pl.multiple_of(own, 8)
    halo = [pl.multiple_of(at, 8) for at in halo]
    own_rows = pl.ds(own, cy)
    ext = (w_ref, r_ref, prev_ref, v_ref)
    even_base, odd_base = 2 * cx * (1 - parity), 2 * cx * parity

    copies = []

    def fetch(src, dst):
        copy = pltpu.make_async_copy(src, dst, sem.at[len(copies)])
        copy.start()
        copies.append(copy)
        return copy

    got_sensors = fetch(arrived_in, arrived_ref)
    got_fields = []
    for field, out in zip(fields, ext):
        for h in halves:
            got_fields.append(fetch(field.at[:, :, half * h : half * (h + 1)], out.at[cx : 2 * cx, h, own_rows]))
    got_halos = [fetch(odd_in, odd_ref), fetch(even_in, even_ref)]
    for n in range(len(sides)):
        own_side, even_side, odd_side = side_in[3 * n : 3 * n + 3]
        for f, out in enumerate(ext):
            for h in halves:
                src = own_side.at[f, :, :, half * h : half * (h + 1)]
                got_fields.append(fetch(src, out.at[cx : 2 * cx, h, pl.ds(halo[n], reach)]))
        got_halos.append(fetch(odd_side, side_refs[2 * n]))
        got_halos.append(fetch(even_side, side_refs[2 * n + 1]))
    got_forward = fetch(forward_in, forward_ref)

    blank = jnp.zeros((3 * cx, 2, pad, half), F32)
    for out in (w_ref, r_ref, prev_ref):
        out[:, :, 0:pad] = blank
        out[:, :, pad + rows : pad + rows + 8] = blank

    width = slots * n_gx
    per = 128 // slots
    lane = iota((8, 128), 1)

    def turned(x, turn):
        return pltpu.roll(x, turn % 128, 1) if turn % 128 else x

    def gathered(strip):
        tiles, codes = [[], [], []], []
        for g0 in range(0, n_gx, per):
            tile, code = [jnp.zeros((8, 128), F32)] * 3, jnp.zeros((8, 128), F32)
            for k in range(per):
                x = arrived_ref[g0 + k, strip]
                here = (lane >= k * slots) & (lane < (k + 1) * slots)
                for slab in range(3):
                    tile[slab] = jnp.where(here, turned(x, (k - slab) * slots), tile[slab])
                code = jnp.where(here, turned(x, (k - 3) * slots), code)
            for slab in range(3):
                tiles[slab].append(tile[slab])
            codes.append(code)
        codes = jnp.concatenate(codes, axis=1)
        return [jnp.concatenate(t, axis=1) for t in tiles], codes.astype(I32) - 1, jnp.transpose(codes).astype(I32) - 1

    def spread(cells_at, amps, column, spans):
        depth = one_hot(iota((width, nz), 1) == (column & (nz - 1)))
        hi, lo = parts_of(amps, 2)
        out = 0.0
        for part in (lo, hi):
            block = jnp.concatenate([cells_at[a:b] * part[t : t + 1] for t, a, b in spans], axis=0)
            out = out + jnp.dot(block, depth, preferred_element_type=F32)
        return out

    for copy in got_fields + got_halos:
        copy.wait()
    for ref, left in ((odd_ref, 1 - parity), (even_ref, parity)):
        base = 2 * cx * (1 - left)
        at = 0
        near = base + (cx - NEAR) * left
        for out, count in zip(ext, plane_counts(cx)):
            first = base + left if count < cx else base
            for h in halves:
                lanes = slice(half * h, half * (h + 1))
                out[pl.ds(first, count), h, own_rows] = ref[at : at + count, :, lanes].astype(F32)
                out[pl.ds(near, NEAR), h, own_rows] += ref[at + count : at + count + NEAR, :, lanes].astype(F32)
            at += count + NEAR
    for n in range(len(sides)):
        upper = side_source(sides[n], j, n_gy, cy, reach)[1] > 0
        at = pl.ds(halo[n], reach)
        mid = cx // 2

        def put(out, x, tile, add=False):
            for h in halves:
                value = tile[:, half * h : half * (h + 1)]
                if add:
                    value = value + out[x, h, at]
                out[x, h, at] = value

        tall = corner_tiles(cx)
        for ref, left in ((side_refs[2 * n], 1 - parity), (side_refs[2 * n + 1], parity)):
            found = tiles_of(ref[...].astype(F32))
            base = 2 * cx * (1 - left)
            for f, out in enumerate(ext):
                tiles = found[f * tall : (f + 1) * tall]
                far = unfold(tiles[mid : mid + mid // 2], upper)
                more = unfold(tiles[mid + mid // 2 :], upper)
                for m in range(mid):
                    put(out, base + mid * left + m, tiles[m])
                    put(out, base + mid * (1 - left) + m, far[m])
                row = iota(more[0].shape, 0)
                nearer = (row >= HALF_ROWS) == upper
                for m in range(NEAR_CORNER):
                    put(out, base + (cx - NEAR_CORNER) * left + m, jnp.where(nearer, more[m], 0.0), add=True)

    got_sensors.wait()
    strips = [(j, None)]
    for side in sides:
        strip, row, there = side_source(side, j, n_gy, cy, reach)
        strips.append((strip, (row, there)))
    for n, (strip, beside) in enumerate(strips):
        amps, codes, columns = gathered(strip)
        tall = cy if beside is None else reach
        at = pl.ds(own - pad if beside is None else halo[n - 1] - pad, tall)
        for slab in range(3):
            code = codes[slab : slab + 1]
            place = code >> 8
            if beside is not None:
                y = (place & (cy - 1)) - beside[0]
                inside = (code >= 0) & (y >= 0) & (y < reach) & beside[1]
                place = jnp.where(inside, (place // cy) * reach + y, -1)
            cells = one_hot(iota((cx * tall, width), 0) == place)
            layers = [(max(t + 1 - cx * slab, 0), min(3 * cx - 1 - t - cx * slab, cx)) for t in range(steps)]
            spans = [(t, a * tall, b * tall) for t, (a, b) in enumerate(layers) if a < b]
            out = spread(cells, amps[slab], columns[:, slab : slab + 1], spans)
            first = 0
            for t, a, b in spans:
                value = out[first : first + b - a].reshape((b - a) // tall, tall, nz)
                first += b - a
                xs = slice(slab * cx + a // tall, slab * cx + b // tall)
                for h in halves:
                    inject[t, xs, h, at] = value[:, :, half * h : half * (h + 1)]

    lane = iota((rows, half), 1)
    last, first = lane == half - 1, lane == 0
    mid, above, below = slice(pad, pad + rows), slice(pad + 1, pad + rows + 1), slice(pad - 1, pad + rows - 1)

    def shifted(x0, x1):
        u0, u1 = pltpu.roll(x0, half - 1, 1), pltpu.roll(x1, half - 1, 1)
        d0, d1 = pltpu.roll(x0, 1, 1), pltpu.roll(x1, 1, 1)
        return (jnp.where(last, u1, u0), u1), (d0, jnp.where(first, d0, d1))

    def over(x):
        return 2.0 / jnp.maximum(x, 1.0)

    def couple(x):
        rho = [r_ref[x, h, mid] for h in halves]
        deep, shallow = shifted(*rho)
        deep = (deep[0], jnp.where(last, 0.0, deep[1]))
        shallow = (jnp.where(first, 0.0, shallow[0]), shallow[1])
        for h in halves:
            vel = 0.11 * v_ref[x, h, mid]
            stiff = vel * vel * rho[h]
            xu, xd = stiff * over(rho[h] + r_ref[x + 1, h, mid]), stiff * over(rho[h] + r_ref[x - 1, h, mid])
            yu, yd = stiff * over(rho[h] + r_ref[x, h, above]), stiff * over(rho[h] + r_ref[x, h, below])
            zu, zd = stiff * over(rho[h] + deep[h]), stiff * over(rho[h] + shallow[h])
            c0[x, h] = 2.0 - (((xu + xd) + (yu + yd)) + (zu + zd))
            cxu[x, h], cxd[x, h], cyu[x, h], cyd[x, h] = xu, xd, yu, yd
            czu[x, h] = jnp.where(last, 0.0, zu) if h == 1 else zu
            czd[x, h] = jnp.where(first, 0.0, zd) if h == 0 else zd

    for x in range(1, 3 * cx - 1):
        couple(x)
    got_forward.wait()

    wave, prev = w_ref, prev_ref
    for t in range(steps):

        def advance(x, wave=wave, prev=prev, t=t):
            w = [wave[x, h, mid] for h in halves]
            deep, shallow = shifted(*w)
            for h in halves:
                u = c0[x, h] * w[h] - prev[x, h, mid] + inject[t, x, h]
                u = u + (cxu[x, h] * wave[x + 1, h, mid] + cxd[x, h] * wave[x - 1, h, mid])
                u = u + (cyu[x, h] * wave[x, h, above] + cyd[x, h] * wave[x, h, below])
                prev[x, h, mid] = u + (czu[x, h] * deep[h] + czd[x, h] * shallow[h])

        def gather(x, prev=prev, t=t):
            for h in halves:
                term = prev[cx + x, h, own_rows] * forward_ref[t, x, :, half * h : half * (h + 1)].astype(F32)
                acc_ref[x, h] = term if t == 0 else acc_ref[x, h] + term

        for x in range(t + 1, 3 * cx - 1 - t):
            advance(x)
            if cx <= x < 2 * cx:
                gather(x - cx)
        wave, prev = prev, wave
    out_copies = [
        fetch(wave.at[cx : 2 * cx, h, own_rows], final_out.at[:, :, half * h : half * (h + 1)]) for h in halves
    ]

    flat = []
    for h in halves:
        blocks = []
        for a in range(0, cx, 2):
            pair = sum((-0.25 / v_ref[cx + b, h, own_rows]) * acc_ref[b, h] for b in (a, a + 1))
            blocks.append(pair)
        flat.append(jnp.concatenate(blocks, axis=0))
    if n_gy == 2:
        flat = [jnp.where(j == h, flat[0], flat[1]) for h in halves]
    half_z = one_hot(iota((half, half // 2), 0) // 2 == iota((half, half // 2), 1))
    count = cx // 2 * cy
    tall = count if n_gy == 2 else count // 2
    to, at = iota((tall, count), 0), iota((tall, count), 1)
    goal = at // cy * cy + j * (cy // 2) + at % cy // 2 if n_gy == 2 else at // 2
    half_y = one_hot(to == goal)
    for h in halves:
        x = sum(jnp.dot(part, half_z, preferred_element_type=F32) for part in parts_of(flat[h], 3)[::-1])
        x = sum(jnp.dot(half_y, part, preferred_element_type=F32) for part in parts_of(x, 3)[::-1])
        if n_gy == 2:
            coarse_refs[h][...] = x.reshape(cx // 2, cy, half // 2)
        else:
            coarse_refs[0][:, half // 2 * h : half // 2 * (h + 1)] = x
    for copy in out_copies:
        copy.wait()


def call(kernel, out_shape, args, scratch=(), in_specs=None, out_specs=None, limit=60 << 20):
    return pl.pallas_call(
        kernel,
        out_shape=out_shape,
        in_specs=in_specs or [VMEM] * len(args),
        out_specs=out_specs or jax.tree.map(lambda _: VMEM, out_shape),
        scratch_shapes=scratch,
        compiler_params=pltpu.CompilerParams(vmem_limit_bytes=limit),
    )(*args)


def shards(
    n_gx,
    n_gy,
    velocity,
    density,
    adjoint_last,
    adjoint_now,
    forward_accel,
    residual_panels,
    owner_slab,
    receiver_cell,
    trace_offset,
):
    cx, cy, nz = velocity.shape
    steps = forward_accel.shape[0]
    reach = steps
    sensors = residual_panels.shape[0]
    slots = sensors // 16
    sides = y_sides(n_gy)
    shape = jax.ShapeDtypeStruct
    fields = (adjoint_now, density, adjoint_last, velocity)

    planes = sum(plane_counts(cx)) + 4 * NEAR
    halo_block = shape((planes, cy, nz), BF16)
    prep_out = [halo_block]
    for _ in sides:
        prep_out += [shape((4, cx, reach, nz), F32)] + [shape((4 * reach * corner_tiles(cx), nz), BF16)] * 2
    sensor_args = (
        residual_panels,
        owner_slab.reshape(1, sensors),
        receiver_cell.reshape(1, sensors),
        trace_offset.reshape(1, sensors),
    )
    stage_args = sensor_args + fields
    stage_out = [shape((n_gx, n_gy, 8, 128), F32)] + prep_out
    odd_send = call(
        odd_kernel,
        halo_block,
        fields,
        [pltpu.VMEM(x.shape, x.dtype) for x in (*fields, halo_block)] + [pltpu.SemaphoreType.DMA((8,))],
        in_specs=[HBM] * 4,
        out_specs=ANY,
    )
    packed, *prep = call(
        functools.partial(stage_kernel, n_gx, n_gy, steps, slots, reach),
        stage_out,
        stage_args,
        [pltpu.VMEM(x.shape, x.dtype) for x in (*stage_args, *stage_out)] + [pltpu.SemaphoreType.DMA((32,))],
        in_specs=[HBM] * len(stage_args),
        out_specs=[ANY] * len(stage_out),
    )
    odd = [(a, a + 1) for a in range(1, n_gx - 1, 2)]
    odd = odd + [(b, a) for a, b in odd]
    even = [(a, a ^ 1) for a in range(n_gx)]
    odd_got = lax.ppermute(odd_send, "gx", odd)
    side_got = []
    for n, side in enumerate(sides):
        if side == "swap":
            over_y = [(0, 1), (1, 0)]
        elif side == "high":
            over_y = [(b + 1, b) for b in range(n_gy - 1)]
        else:
            over_y = [(b, b + 1) for b in range(n_gy - 1)]
        corner = [(a * n_gy + c, b * n_gy + d) for a, b in odd for c, d in over_y]
        own_side = lax.ppermute(prep[1 + 3 * n], "gy", over_y)
        odd_side = lax.ppermute(prep[2 + 3 * n], ("gx", "gy"), corner)
        corner = [(a * n_gy + c, b * n_gy + d) for a, b in even for c, d in over_y]
        even_side = lax.ppermute(prep[3 + 3 * n], ("gx", "gy"), corner)
        side_got.append((own_side, even_side, odd_side))
    even_got = lax.ppermute(prep[0], "gx", even)

    arrived = lax.all_to_all(
        packed.reshape(n_gx * n_gy, 8, 128), ("gx", "gy"), split_axis=0, concat_axis=0, tiled=True
    ).reshape(n_gx, n_gy, 8, 128)
    side_args = [x for got in side_got for x in got]

    rows = cy + reach * len(sides)
    padded = pltpu.VMEM((3 * cx, 2, rows + 16, nz // 2), F32)
    block = pltpu.VMEM((3 * cx, 2, rows, nz // 2), F32)
    if n_gy == 2:
        outs = [shape((cx // 2, cy, nz // 4), F32)] * 2
    else:
        outs = [shape((cx * cy // 4, nz // 2), F32)]
    buffers = [forward_accel, arrived, odd_got, even_got] + [x for got in side_got for x in (got[2], got[1])]
    got = call(
        functools.partial(sim_kernel, n_gx, n_gy, steps, slots, reach),
        [shape((cx, cy, nz), F32)] + outs,
        fields + (forward_accel, arrived, odd_got, even_got) + tuple(side_args),
        [padded] * 4
        + [block] * 7
        + [pltpu.VMEM((steps, 3 * cx, 2, rows, nz // 2), F32), pltpu.VMEM((cx, 2, cy, nz // 2), F32)]
        + [pltpu.VMEM(x.shape, x.dtype) for x in buffers]
        + [pltpu.SemaphoreType.DMA((64,))],
        in_specs=[HBM] * 5 + [ANY] * (3 + len(side_args)),
        out_specs=[HBM] + [VMEM] * len(outs),
        limit=50 << 20,
    )
    if n_gy == 2:
        final, mine, send = got
        whole = mine + lax.ppermute(send, "gy", [(0, 1), (1, 0)])
        sensitivity = jnp.transpose(whole, (0, 2, 1))
    else:
        final, coarse = got
        coarse = jnp.transpose(coarse.reshape(cx // 2, cy // 2, nz // 2), (0, 2, 1))
        sensitivity = lax.all_to_all(coarse, "gy", split_axis=1, concat_axis=2, tiled=True)
    return sensitivity, final


def solution(mesh):
    in_specs = (
        P("gx", "gy", None),
        P("gx", "gy", None),
        P("gx", "gy", None),
        P("gx", "gy", None),
        P(None, "gx", "gy", None),
        P(("gx", "gy"), None),
        P(("gx", "gy"), None),
        P(("gx", "gy")),
        P(("gx", "gy")),
    )
    out_specs = (P("gx", "gy", None), P("gx", "gy", None))
    body = functools.partial(shards, mesh.shape["gx"], mesh.shape["gy"])
    return jax.shard_map(body, mesh=mesh, in_specs=in_specs, out_specs=out_specs, check_vma=False)
```

```python
import functools

import jax
import jax.numpy as jnp
from jax import lax
from jax.experimental import pallas as pl
from jax.experimental.pallas import tpu as pltpu
from jax.sharding import PartitionSpec as P

F32, BF16, I32 = jnp.float32, jnp.bfloat16, jnp.int32
NEAR = 3
NEAR_CORNER = 2
HALF_ROWS = 4
VMEM = pl.BlockSpec(memory_space=pltpu.VMEM)
ANY = pl.BlockSpec(memory_space=pl.ANY)
HBM = pl.BlockSpec(memory_space=pltpu.HBM)


def iota(shape, dim):
    return lax.broadcasted_iota(I32, shape, dim)


def dot_t(a, b):
    return lax.dot_general(a, b, (((1,), (1,)), ((), ())), preferred_element_type=F32)


def parts_of(x, count):
    parts = []
    for _ in range(count):
        part = x.astype(BF16)
        parts.append(part)
        x = x - part.astype(F32)
    return parts


def one_hot(flags):
    return jnp.where(flags, 1.0, 0.0).astype(BF16)


def y_sides(n_gy):
    return ("swap",) if n_gy == 2 else ("high", "low")


def send_row(side, j, cy, reach):
    if side == "swap":
        return (cy - reach) * (1 - j)
    return 0 if side == "high" else cy - reach


def side_source(side, j, n_gy, cy, reach):
    if side == "swap":
        return 1 - j, (cy - reach) * j, j >= 0
    if side == "high":
        return jnp.minimum(j + 1, n_gy - 1), 0, j + 1 < n_gy
    return jnp.maximum(j - 1, 0), cy - reach, j > 0


def pack_kernel(n_gx, n_gy, steps, slots, panels_ref, owner_ref, cell_ref, offset_ref, out_ref):
    sensors, length = panels_ref.shape
    half = length // steps
    span = 2 * half
    row, sample = iota((span * steps, length), 0), iota((span * steps, length), 1)
    clock = (sample + row // steps).astype(F32)
    centre = ((row % steps + 1) * half).astype(F32)
    weights = jnp.maximum(0.0, 1.0 - jnp.abs(clock - centre) * (1.0 / half)) * 0.25
    shifted = dot_t(weights.astype(BF16), panels_ref[...])
    offsets = offset_ref[...]
    amplitudes = jnp.zeros((steps, sensors), F32)
    for o in range(span):
        amplitudes = jnp.where(offsets == o, shifted[o * steps : (o + 1) * steps], amplitudes)
    owners = owner_ref[...]
    named = iota((n_gx, sensors), 0) == owners
    earlier = one_hot(iota((sensors, sensors), 0) <= iota((sensors, sensors), 1))
    counts = jnp.dot(one_hot(named), earlier, preferred_element_type=F32)
    rank = jnp.sum(jnp.where(named, counts, 0.0), axis=0, keepdims=True).astype(I32) - 1
    target = owners * slots + rank
    places = n_gx * slots
    moved = one_hot(iota((places, sensors), 0) == target)
    code = cell_ref[...] + 1
    line = iota((8, sensors), 0)
    code_rows = jnp.where(line == 0, code >> 8, jnp.where(line == 1, code & 255, 0))
    rows = parts_of(amplitudes, 3) + [code_rows.astype(F32).astype(BF16)]
    packed = [dot_t(part, moved) for part in rows]
    packed_amp = packed[0] + packed[1] + packed[2]
    packed_code = packed[3][0:1] * 256.0 + packed[3][1:2]
    blank = jnp.zeros((8, 128), F32)
    width = places + 128
    amp_pad = pltpu.roll(jnp.concatenate([packed_amp, blank], axis=1), slots, 1)
    code_pad = jnp.concatenate([jnp.broadcast_to(packed_code, (8, places)), blank], axis=1)
    code_pad = pltpu.roll(code_pad, slots, 1)
    line = iota((8, width), 0)
    lines = jnp.zeros((8, width), F32)
    for r in range(3):
        lines = jnp.where(line == r, pltpu.roll(code_pad, (3 - r) * slots, 1), lines)
    lane = iota((8, 128), 1)
    for g in range(n_gx):
        at = (g * slots) // 128 * 128
        turn = (256 - (g * slots) % 128) % 256
        if at + 256 <= width:
            amp_window, code_window = amp_pad[:, at : at + 256], lines[:, at : at + 256]
            if turn:
                amp_window, code_window = pltpu.roll(amp_window, turn, 1), pltpu.roll(code_window, turn, 1)
        else:
            amp_window, code_window = amp_pad[:, at : at + 128], lines[:, at : at + 128]
        tile = jnp.where(lane < 3 * slots, amp_window[:, :128], code_window[:, :128])
        for j in range(n_gy):
            out_ref[g, j] = tile


def plane_counts(cx):
    return (cx, cx, cx - 1, cx - 1)


def halo_planes(x_ref, out_ref, at, count, right):
    cx = x_ref.shape[0]
    first = right if count < cx else 0
    out_ref[at : at + count] = x_ref[pl.ds(first, count)].astype(BF16)
    x = x_ref[pl.ds((cx - NEAR) * right, NEAR)]
    out_ref[at + count : at + count + NEAR] = (x - x.astype(BF16).astype(F32)).astype(BF16)


def odd_kernel(*refs):
    given, out, held, made, sem = refs[:4], refs[4], refs[5:9], refs[9], refs[10]
    parity = lax.rem(lax.axis_index("gx"), 2)
    copies = [pltpu.make_async_copy(src, dst, sem.at[n]) for n, (src, dst) in enumerate(zip(given, held))]
    for copy in copies:
        copy.start()
    at, sent = 0, []
    for n, count in enumerate(plane_counts(held[0].shape[0])):
        copies[n].wait()
        halo_planes(held[n], made, at, count, parity)
        planes = pl.ds(at, count + NEAR)
        sent.append(pltpu.make_async_copy(made.at[planes], out.at[planes], sem.at[4 + n]))
        sent[-1].start()
        at += count + NEAR
    for copy in sent:
        copy.wait()


def second(x):
    return x - x.astype(BF16).astype(F32)


def fold(x, upper):
    up = jnp.where(upper, 1, 0)
    x = [x[n] for n in range(x.shape[0])]
    turned = [pltpu.roll(y, HALF_ROWS, 0) for y in x]
    row = iota(x[0].shape, 0)
    pairs = []
    for n in range(0, len(x), 2):
        later = jnp.where(up == 1, x[n], turned[n])
        sooner = jnp.where(up == 1, turned[n + 1], x[n + 1])
        pairs.append(jnp.where(row < HALF_ROWS, sooner, later))
    return pairs


def unfold(pairs, upper):
    up = jnp.where(upper, 1, 0)
    layers = []
    for y in pairs:
        turned = pltpu.roll(y, HALF_ROWS, 0)
        layers += [jnp.where(up == 1, y, turned), jnp.where(up == 1, turned, y)]
    return layers


def corner_tiles(cx):
    return cx // 2 + (cx // 2 + NEAR_CORNER) // 2


def tiles_of(x):
    return [x[n : n + 8] for n in range(0, x.shape[0], 8)]


def side_kernel(n_gy, reach, now_ref, rho_ref, last_ref, vel_ref, even_ref, *side_refs, done):
    cx, cy, nz = now_ref.shape
    i, j = lax.axis_index("gx"), lax.axis_index("gy")
    parity = lax.rem(i, 2)
    fields = (now_ref, rho_ref, last_ref, vel_ref)
    for n, side in enumerate(y_sides(n_gy)):
        row = send_row(side, j, cy, reach)
        rows = pl.ds(pl.multiple_of(row, reach), reach)
        y_ref, odd_ref, even_corner_ref = side_refs[3 * n : 3 * n + 3]
        upper = row > 0
        blocks = [[], []]
        mid = cx // 2
        for f, ref in enumerate(fields):
            y_ref[f] = ref[:, rows, :]
            for block, right in ((blocks[0], parity), (blocks[1], 1 - parity)):
                near = ref[pl.ds(mid * right, mid), rows, :]
                block += [near[m] for m in range(mid)]
                block += fold(ref[pl.ds(mid * (1 - right), mid), rows, :], upper)
                block += fold(second(ref[pl.ds((cx - NEAR_CORNER) * right, NEAR_CORNER), rows, :]), upper)
        for out_ref, block in zip((odd_ref, even_corner_ref), blocks):
            out_ref[...] = jnp.concatenate(block, axis=0).astype(BF16)
        for m in range(3):
            done(1 + 3 * n + m)
    at = 0
    for ref, count in zip(fields, plane_counts(cx)):
        halo_planes(ref, even_ref, at, count, 1 - parity)
        at += count + NEAR
    done(0)


def stage_kernel(n_gx, n_gy, steps, slots, reach, *refs):
    given, refs = refs[:8], refs[8:]
    count = 2 + 3 * len(y_sides(n_gy))
    outs, refs = refs[:count], refs[count:]
    held, made, sem = refs[:8], refs[8 : 8 + count], refs[8 + count]
    copies_in = [pltpu.make_async_copy(src, dst, sem.at[n]) for n, (src, dst) in enumerate(zip(given, held))]
    copies_out = [pltpu.make_async_copy(src, dst, sem.at[8 + n]) for n, (src, dst) in enumerate(zip(made, outs))]
    for copy in copies_in:
        copy.start()
    for copy in copies_in[:4]:
        copy.wait()
    pack_kernel(n_gx, n_gy, steps, slots, *held[:4], made[0])
    copies_out[0].start()
    for copy in copies_in[4:]:
        copy.wait()
    side_kernel(n_gy, reach, *held[4:], *made[1:], done=lambda n: copies_out[1 + n].start())
    for copy in copies_out:
        copy.wait()


def sim_kernel(n_gx, n_gy, steps, slots, reach, *refs):
    sides = y_sides(n_gy)
    fields, forward_in, arrived_in, odd_in, even_in = refs[:4], *refs[4:8]
    side_in = refs[8 : 8 + 3 * len(sides)]
    refs = refs[8 + 3 * len(sides) :]
    final_out = refs[0]
    coarse_refs, refs = (refs[1:3], refs[3:]) if n_gy == 2 else (refs[1:2], refs[2:])
    (w_ref, r_ref, prev_ref, v_ref, c0, cxu, cxd, cyu, cyd, czu, czd, inject, acc_ref), refs = refs[:13], refs[13:]
    forward_ref, arrived_ref, odd_ref, even_ref, *side_refs, sem = refs
    cx, cy, nz = fields[0].shape
    half = nz // 2
    halves = range(2)
    rows = cy + reach * len(sides)
    pad = 8
    i, j = lax.axis_index("gx"), lax.axis_index("gy")
    parity = lax.rem(i, 2)
    if n_gy == 2:
        own, halo = pad + reach * j, (pad + cy * (1 - j),)
    else:
        own, halo = pad + reach, (pad + reach + cy, pad)
    own = pl.multiple_of(own, 8)
    halo = [pl.multiple_of(at, 8) for at in halo]
    own_rows = pl.ds(own, cy)
    ext = (w_ref, r_ref, prev_ref, v_ref)
    even_base, odd_base = 2 * cx * (1 - parity), 2 * cx * parity

    copies = []

    def fetch(src, dst):
        copy = pltpu.make_async_copy(src, dst, sem.at[len(copies)])
        copy.start()
        copies.append(copy)
        return copy

    got_sensors = fetch(arrived_in, arrived_ref)
    got_fields = []
    for field, out in zip(fields, ext):
        for h in halves:
            got_fields.append(fetch(field.at[:, :, half * h : half * (h + 1)], out.at[cx : 2 * cx, h, own_rows]))
    got_halos = [fetch(odd_in, odd_ref), fetch(even_in, even_ref)]
    for n in range(len(sides)):
        own_side, even_side, odd_side = side_in[3 * n : 3 * n + 3]
        for f, out in enumerate(ext):
            for h in halves:
                src = own_side.at[f, :, :, half * h : half * (h + 1)]
                got_fields.append(fetch(src, out.at[cx : 2 * cx, h, pl.ds(halo[n], reach)]))
        got_halos.append(fetch(odd_side, side_refs[2 * n]))
        got_halos.append(fetch(even_side, side_refs[2 * n + 1]))
    got_forward = fetch(forward_in, forward_ref)

    blank = jnp.zeros((3 * cx, 2, pad, half), F32)
    for out in (w_ref, r_ref, prev_ref):
        out[:, :, 0:pad] = blank
        out[:, :, pad + rows : pad + rows + 8] = blank

    width = slots * n_gx
    per = 128 // slots
    lane = iota((8, 128), 1)

    def turned(x, turn):
        return pltpu.roll(x, turn % 128, 1) if turn % 128 else x

    def gathered(strip):
        tiles, codes = [[], [], []], []
        for g0 in range(0, n_gx, per):
            tile, code = [jnp.zeros((8, 128), F32)] * 3, jnp.zeros((8, 128), F32)
            for k in range(per):
                x = arrived_ref[g0 + k, strip]
                here = (lane >= k * slots) & (lane < (k + 1) * slots)
                for slab in range(3):
                    tile[slab] = jnp.where(here, turned(x, (k - slab) * slots), tile[slab])
                code = jnp.where(here, turned(x, (k - 3) * slots), code)
            for slab in range(3):
                tiles[slab].append(tile[slab])
            codes.append(code)
        codes = jnp.concatenate(codes, axis=1)
        return [jnp.concatenate(t, axis=1) for t in tiles], codes.astype(I32) - 1, jnp.transpose(codes).astype(I32) - 1

    def spread(cells_at, amps, column, spans, near_spans):
        depth = one_hot(iota((width, nz), 1) == (column & (nz - 1)))
        outs = []
        for part, chosen in zip(parts_of(amps, 2), (spans, near_spans)):
            block = jnp.concatenate([cells_at[a:b] * part[t : t + 1] for t, a, b in chosen], axis=0)
            outs.append(jnp.dot(block, depth, preferred_element_type=F32))
        values, first, first_near = [], 0, 0
        nearer = {t: (a, b) for t, a, b in near_spans}
        for t, a, b in spans:
            c, d = nearer[t]
            x = outs[0][first : first + b - a]
            y = x[c - a : d - a] + outs[1][first_near : first_near + d - c]
            values.append(jnp.concatenate([z for z in (x[: c - a], y, x[d - a :]) if z.shape[0]], axis=0))
            first, first_near = first + b - a, first_near + d - c
        return values

    for copy in got_fields + got_halos:
        copy.wait()
    for ref, left in ((odd_ref, 1 - parity), (even_ref, parity)):
        base = 2 * cx * (1 - left)
        at = 0
        near = base + (cx - NEAR) * left
        for out, count in zip(ext, plane_counts(cx)):
            first = base + left if count < cx else base
            for h in halves:
                lanes = slice(half * h, half * (h + 1))
                out[pl.ds(first, count), h, own_rows] = ref[at : at + count, :, lanes].astype(F32)
                out[pl.ds(near, NEAR), h, own_rows] += ref[at + count : at + count + NEAR, :, lanes].astype(F32)
            at += count + NEAR
    for n in range(len(sides)):
        upper = side_source(sides[n], j, n_gy, cy, reach)[1] > 0
        at = pl.ds(halo[n], reach)
        mid = cx // 2

        def put(out, x, tile, add=False):
            for h in halves:
                value = tile[:, half * h : half * (h + 1)]
                if add:
                    value = value + out[x, h, at]
                out[x, h, at] = value

        tall = corner_tiles(cx)
        for ref, left in ((side_refs[2 * n], 1 - parity), (side_refs[2 * n + 1], parity)):
            found = tiles_of(ref[...].astype(F32))
            base = 2 * cx * (1 - left)
            for f, out in enumerate(ext):
                tiles = found[f * tall : (f + 1) * tall]
                far = unfold(tiles[mid : mid + mid // 2], upper)
                more = unfold(tiles[mid + mid // 2 :], upper)
                for m in range(mid):
                    put(out, base + mid * left + m, tiles[m])
                    put(out, base + mid * (1 - left) + m, far[m])
                row = iota(more[0].shape, 0)
                nearer = (row >= HALF_ROWS) == upper
                for m in range(NEAR_CORNER):
                    put(out, base + (cx - NEAR_CORNER) * left + m, jnp.where(nearer, more[m], 0.0), add=True)

    got_sensors.wait()
    strips = [(j, None)]
    for side in sides:
        strip, row, there = side_source(side, j, n_gy, cy, reach)
        strips.append((strip, (row, there)))
    for n, (strip, beside) in enumerate(strips):
        amps, codes, columns = gathered(strip)
        tall = cy if beside is None else reach
        at = pl.ds(own - pad if beside is None else halo[n - 1] - pad, tall)
        for slab in range(3):
            code = codes[slab : slab + 1]
            place = code >> 8
            if beside is not None:
                y = (place & (cy - 1)) - beside[0]
                inside = (code >= 0) & (y >= 0) & (y < reach) & beside[1]
                place = jnp.where(inside, (place // cy) * reach + y, -1)
            cells = one_hot(iota((cx * tall, width), 0) == place)
            layers = [(max(t + 1 - cx * slab, 0), min(3 * cx - 1 - t - cx * slab, cx)) for t in range(steps)]
            spans = [(t, a * tall, b * tall) for t, (a, b) in enumerate(layers) if a < b]
            low, high = ((cx - NEAR) * tall, cx * tall) if slab == 0 else (0, (cx if slab == 1 else NEAR) * tall)
            near_spans = [(t, min(max(a, low), b), max(min(b, high), a)) for t, a, b in spans]
            values = spread(cells, amps[slab], columns[:, slab : slab + 1], spans, near_spans)
            for (t, a, b), value in zip(spans, values):
                value = value.reshape((b - a) // tall, tall, nz)
                xs = slice(slab * cx + a // tall, slab * cx + b // tall)
                for h in halves:
                    inject[t, xs, h, at] = value[:, :, half * h : half * (h + 1)]

    lane = iota((rows, half), 1)
    last, first = lane == half - 1, lane == 0
    mid, above, below = slice(pad, pad + rows), slice(pad + 1, pad + rows + 1), slice(pad - 1, pad + rows - 1)

    def shifted(x0, x1):
        u0, u1 = pltpu.roll(x0, half - 1, 1), pltpu.roll(x1, half - 1, 1)
        d0, d1 = pltpu.roll(x0, 1, 1), pltpu.roll(x1, 1, 1)
        return (jnp.where(last, u1, u0), u1), (d0, jnp.where(first, d0, d1))

    def over(x):
        return 2.0 / jnp.maximum(x, 1.0)

    def couple(x):
        rho = [r_ref[x, h, mid] for h in halves]
        deep, shallow = shifted(*rho)
        deep = (deep[0], jnp.where(last, 0.0, deep[1]))
        shallow = (jnp.where(first, 0.0, shallow[0]), shallow[1])
        for h in halves:
            vel = 0.11 * v_ref[x, h, mid]
            stiff = vel * vel * rho[h]
            xu, xd = stiff * over(rho[h] + r_ref[x + 1, h, mid]), stiff * over(rho[h] + r_ref[x - 1, h, mid])
            yu, yd = stiff * over(rho[h] + r_ref[x, h, above]), stiff * over(rho[h] + r_ref[x, h, below])
            zu, zd = stiff * over(rho[h] + deep[h]), stiff * over(rho[h] + shallow[h])
            c0[x, h] = 2.0 - (((xu + xd) + (yu + yd)) + (zu + zd))
            cxu[x, h], cxd[x, h], cyu[x, h], cyd[x, h] = xu, xd, yu, yd
            czu[x, h] = jnp.where(last, 0.0, zu) if h == 1 else zu
            czd[x, h] = jnp.where(first, 0.0, zd) if h == 0 else zd

    for x in range(1, 3 * cx - 1):
        couple(x)
    got_forward.wait()

    wave, prev = w_ref, prev_ref
    for t in range(steps):

        def advance(x, w, behind, wave=wave, prev=prev, t=t):
            ahead = [wave[x + 1, h, mid] for h in halves]
            deep, shallow = shifted(*w)
            for h in halves:
                u = c0[x, h] * w[h] - prev[x, h, mid] + inject[t, x, h]
                u = u + (cxu[x, h] * ahead[h] + cxd[x, h] * behind[h])
                u = u + (cyu[x, h] * wave[x, h, above] + cyd[x, h] * wave[x, h, below])
                prev[x, h, mid] = u + (czu[x, h] * deep[h] + czd[x, h] * shallow[h])
            return ahead, w

        def gather(x, prev=prev, t=t):
            for h in halves:
                term = prev[cx + x, h, own_rows] * forward_ref[t, x, :, half * h : half * (h + 1)].astype(F32)
                acc_ref[x, h] = term if t == 0 else acc_ref[x, h] + term

        at, behind = [wave[t + 1, h, mid] for h in halves], [wave[t, h, mid] for h in halves]
        for x in range(t + 1, 3 * cx - 1 - t):
            at, behind = advance(x, at, behind)
            if cx <= x < 2 * cx:
                gather(x - cx)
        wave, prev = prev, wave
    out_copies = [
        fetch(wave.at[cx : 2 * cx, h, own_rows], final_out.at[:, :, half * h : half * (h + 1)]) for h in halves
    ]

    flat = []
    for h in halves:
        blocks = []
        for a in range(0, cx, 2):
            pair = sum((-0.25 / v_ref[cx + b, h, own_rows]) * acc_ref[b, h] for b in (a, a + 1))
            blocks.append(pair)
        flat.append(jnp.concatenate(blocks, axis=0))
    if n_gy == 2:
        flat = [jnp.where(j == h, flat[0], flat[1]) for h in halves]
    half_z = one_hot(iota((half, half // 2), 0) // 2 == iota((half, half // 2), 1))
    count = cx // 2 * cy
    tall = count if n_gy == 2 else count // 2
    to, at = iota((tall, count), 0), iota((tall, count), 1)
    goal = at // cy * cy + j * (cy // 2) + at % cy // 2 if n_gy == 2 else at // 2
    half_y = one_hot(to == goal)
    for h in halves:
        x = sum(jnp.dot(part, half_z, preferred_element_type=F32) for part in parts_of(flat[h], 3)[::-1])
        x = sum(jnp.dot(half_y, part, preferred_element_type=F32) for part in parts_of(x, 3)[::-1])
        if n_gy == 2:
            coarse_refs[h][...] = x.reshape(cx // 2, cy, half // 2)
        else:
            coarse_refs[0][:, half // 2 * h : half // 2 * (h + 1)] = x
    for copy in out_copies:
        copy.wait()


def call(kernel, out_shape, args, scratch=(), in_specs=None, out_specs=None, limit=60 << 20):
    return pl.pallas_call(
        kernel,
        out_shape=out_shape,
        in_specs=in_specs or [VMEM] * len(args),
        out_specs=out_specs or jax.tree.map(lambda _: VMEM, out_shape),
        scratch_shapes=scratch,
        compiler_params=pltpu.CompilerParams(vmem_limit_bytes=limit),
    )(*args)


def shards(
    n_gx,
    n_gy,
    velocity,
    density,
    adjoint_last,
    adjoint_now,
    forward_accel,
    residual_panels,
    owner_slab,
    receiver_cell,
    trace_offset,
):
    cx, cy, nz = velocity.shape
    steps = forward_accel.shape[0]
    reach = steps
    sensors = residual_panels.shape[0]
    slots = sensors // 16
    sides = y_sides(n_gy)
    shape = jax.ShapeDtypeStruct
    fields = (adjoint_now, density, adjoint_last, velocity)

    planes = sum(plane_counts(cx)) + 4 * NEAR
    halo_block = shape((planes, cy, nz), BF16)
    prep_out = [halo_block]
    for _ in sides:
        prep_out += [shape((4, cx, reach, nz), F32)] + [shape((4 * reach * corner_tiles(cx), nz), BF16)] * 2
    sensor_args = (
        residual_panels,
        owner_slab.reshape(1, sensors),
        receiver_cell.reshape(1, sensors),
        trace_offset.reshape(1, sensors),
    )
    stage_args = sensor_args + fields
    stage_out = [shape((n_gx, n_gy, 8, 128), F32)] + prep_out
    odd_send = call(
        odd_kernel,
        halo_block,
        fields,
        [pltpu.VMEM(x.shape, x.dtype) for x in (*fields, halo_block)] + [pltpu.SemaphoreType.DMA((8,))],
        in_specs=[HBM] * 4,
        out_specs=ANY,
    )
    packed, *prep = call(
        functools.partial(stage_kernel, n_gx, n_gy, steps, slots, reach),
        stage_out,
        stage_args,
        [pltpu.VMEM(x.shape, x.dtype) for x in (*stage_args, *stage_out)] + [pltpu.SemaphoreType.DMA((32,))],
        in_specs=[HBM] * len(stage_args),
        out_specs=[ANY] * len(stage_out),
    )
    odd = [(a, a + 1) for a in range(1, n_gx - 1, 2)]
    odd = odd + [(b, a) for a, b in odd]
    even = [(a, a ^ 1) for a in range(n_gx)]
    odd_got = lax.ppermute(odd_send, "gx", odd)
    side_got = []
    for n, side in enumerate(sides):
        if side == "swap":
            over_y = [(0, 1), (1, 0)]
        elif side == "high":
            over_y = [(b + 1, b) for b in range(n_gy - 1)]
        else:
            over_y = [(b, b + 1) for b in range(n_gy - 1)]
        corner = [(a * n_gy + c, b * n_gy + d) for a, b in odd for c, d in over_y]
        own_side = lax.ppermute(prep[1 + 3 * n], "gy", over_y)
        odd_side = lax.ppermute(prep[2 + 3 * n], ("gx", "gy"), corner)
        corner = [(a * n_gy + c, b * n_gy + d) for a, b in even for c, d in over_y]
        even_side = lax.ppermute(prep[3 + 3 * n], ("gx", "gy"), corner)
        side_got.append((own_side, even_side, odd_side))
    even_got = lax.ppermute(prep[0], "gx", even)

    arrived = lax.all_to_all(
        packed.reshape(n_gx * n_gy, 8, 128), ("gx", "gy"), split_axis=0, concat_axis=0, tiled=True
    ).reshape(n_gx, n_gy, 8, 128)
    side_args = [x for got in side_got for x in got]

    rows = cy + reach * len(sides)
    padded = pltpu.VMEM((3 * cx, 2, rows + 16, nz // 2), F32)
    block = pltpu.VMEM((3 * cx, 2, rows, nz // 2), F32)
    if n_gy == 2:
        outs = [shape((cx // 2, cy, nz // 4), F32)] * 2
    else:
        outs = [shape((cx * cy // 4, nz // 2), F32)]
    buffers = [forward_accel, arrived, odd_got, even_got] + [x for got in side_got for x in (got[2], got[1])]
    got = call(
        functools.partial(sim_kernel, n_gx, n_gy, steps, slots, reach),
        [shape((cx, cy, nz), F32)] + outs,
        fields + (forward_accel, arrived, odd_got, even_got) + tuple(side_args),
        [padded] * 4
        + [block] * 7
        + [pltpu.VMEM((steps, 3 * cx, 2, rows, nz // 2), F32), pltpu.VMEM((cx, 2, cy, nz // 2), F32)]
        + [pltpu.VMEM(x.shape, x.dtype) for x in buffers]
        + [pltpu.SemaphoreType.DMA((64,))],
        in_specs=[HBM] * 5 + [ANY] * (3 + len(side_args)),
        out_specs=[HBM] + [VMEM] * len(outs),
        limit=50 << 20,
    )
    if n_gy == 2:
        final, mine, send = got
        whole = mine + lax.ppermute(send, "gy", [(0, 1), (1, 0)])
        sensitivity = jnp.transpose(whole, (0, 2, 1))
    else:
        final, coarse = got
        coarse = jnp.transpose(coarse.reshape(cx // 2, cy // 2, nz // 2), (0, 2, 1))
        sensitivity = lax.all_to_all(coarse, "gy", split_axis=1, concat_axis=2, tiled=True)
    return sensitivity, final


def solution(mesh):
    in_specs = (
        P("gx", "gy", None),
        P("gx", "gy", None),
        P("gx", "gy", None),
        P("gx", "gy", None),
        P(None, "gx", "gy", None),
        P(("gx", "gy"), None),
        P(("gx", "gy"), None),
        P(("gx", "gy")),
        P(("gx", "gy")),
    )
    out_specs = (P("gx", "gy", None), P("gx", "gy", None))
    body = functools.partial(shards, mesh.shape["gx"], mesh.shape["gy"])
    return jax.shard_map(body, mesh=mesh, in_specs=in_specs, out_specs=out_specs, check_vma=False)
```

```python
import functools

import jax
import jax.numpy as jnp
from jax import lax
from jax.experimental import pallas as pl
from jax.experimental.pallas import tpu as pltpu
from jax.sharding import PartitionSpec as P

F32, BF16, I32 = jnp.float32, jnp.bfloat16, jnp.int32
NEAR = 3
NEAR_CORNER = 2
HALF_ROWS = 4
VMEM = pl.BlockSpec(memory_space=pltpu.VMEM)
ANY = pl.BlockSpec(memory_space=pl.ANY)
HBM = pl.BlockSpec(memory_space=pltpu.HBM)


def iota(shape, dim):
    return lax.broadcasted_iota(I32, shape, dim)


def dot_t(a, b):
    return lax.dot_general(a, b, (((1,), (1,)), ((), ())), preferred_element_type=F32)


def parts_of(x, count):
    parts = []
    for _ in range(count):
        part = x.astype(BF16)
        parts.append(part)
        x = x - part.astype(F32)
    return parts


def one_hot(flags):
    return jnp.where(flags, 1.0, 0.0).astype(BF16)


def y_sides(n_gy):
    return ("swap",) if n_gy == 2 else ("high", "low")


def send_row(side, j, cy, reach):
    if side == "swap":
        return (cy - reach) * (1 - j)
    return 0 if side == "high" else cy - reach


def side_source(side, j, n_gy, cy, reach):
    if side == "swap":
        return 1 - j, (cy - reach) * j, j >= 0
    if side == "high":
        return jnp.minimum(j + 1, n_gy - 1), 0, j + 1 < n_gy
    return jnp.maximum(j - 1, 0), cy - reach, j > 0


def pack_kernel(n_gx, n_gy, steps, slots, panels_ref, owner_ref, cell_ref, offset_ref, out_ref):
    sensors, length = panels_ref.shape
    half = length // steps
    span = 2 * half
    row, sample = iota((span * steps, length), 0), iota((span * steps, length), 1)
    clock = (sample + row // steps).astype(F32)
    centre = ((row % steps + 1) * half).astype(F32)
    weights = jnp.maximum(0.0, 1.0 - jnp.abs(clock - centre) * (1.0 / half)) * 0.25
    shifted = dot_t(weights.astype(BF16), panels_ref[...])
    offsets = offset_ref[...]
    amplitudes = jnp.zeros((steps, sensors), F32)
    for o in range(span):
        amplitudes = jnp.where(offsets == o, shifted[o * steps : (o + 1) * steps], amplitudes)
    owners = owner_ref[...]
    named = iota((n_gx, sensors), 0) == owners
    earlier = one_hot(iota((sensors, sensors), 0) <= iota((sensors, sensors), 1))
    counts = jnp.dot(one_hot(named), earlier, preferred_element_type=F32)
    rank = jnp.sum(jnp.where(named, counts, 0.0), axis=0, keepdims=True).astype(I32) - 1
    target = owners * slots + rank
    places = n_gx * slots
    moved = one_hot(iota((places, sensors), 0) == target)
    code = cell_ref[...] + 1
    line = iota((8, sensors), 0)
    code_rows = jnp.where(line == 0, code >> 8, jnp.where(line == 1, code & 255, 0))
    rows = [part.astype(F32) for part in parts_of(amplitudes, 3)] + [code_rows.astype(F32)]
    packed = dot_t(jnp.concatenate(rows, axis=0).astype(BF16), moved)
    packed_amp = packed[0:8] + packed[8:16] + packed[16:24]
    packed_code = packed[24:25] * 256.0 + packed[25:26]
    blank = jnp.zeros((8, 128), F32)
    width = places + 128
    amp_pad = pltpu.roll(jnp.concatenate([packed_amp, blank], axis=1), slots, 1)
    code_pad = jnp.concatenate([jnp.broadcast_to(packed_code, (8, places)), blank], axis=1)
    code_pad = pltpu.roll(code_pad, slots, 1)
    line = iota((8, width), 0)
    lines = jnp.zeros((8, width), F32)
    for r in range(3):
        lines = jnp.where(line == r, pltpu.roll(code_pad, (3 - r) * slots, 1), lines)
    lane = iota((8, 128), 1)
    for g in range(n_gx):
        at = (g * slots) // 128 * 128
        turn = (256 - (g * slots) % 128) % 256
        if at + 256 <= width:
            amp_window, code_window = amp_pad[:, at : at + 256], lines[:, at : at + 256]
            if turn:
                amp_window, code_window = pltpu.roll(amp_window, turn, 1), pltpu.roll(code_window, turn, 1)
        else:
            amp_window, code_window = amp_pad[:, at : at + 128], lines[:, at : at + 128]
        tile = jnp.where(lane < 3 * slots, amp_window[:, :128], code_window[:, :128])
        for j in range(n_gy):
            out_ref[g, j] = tile


def plane_counts(cx):
    return (cx, cx, cx - 1, cx - 1)


def halo_planes(x_ref, out_ref, at, count, right):
    cx = x_ref.shape[0]
    first = right if count < cx else 0
    out_ref[at : at + count] = x_ref[pl.ds(first, count)].astype(BF16)
    x = x_ref[pl.ds((cx - NEAR) * right, NEAR)]
    out_ref[at + count : at + count + NEAR] = (x - x.astype(BF16).astype(F32)).astype(BF16)


def odd_kernel(*refs):
    given, out, held, made, sem = refs[:4], refs[4], refs[5:9], refs[9], refs[10]
    parity = lax.rem(lax.axis_index("gx"), 2)
    copies = [pltpu.make_async_copy(src, dst, sem.at[n]) for n, (src, dst) in enumerate(zip(given, held))]
    for copy in copies:
        copy.start()
    at, sent = 0, []
    for n, count in enumerate(plane_counts(held[0].shape[0])):
        copies[n].wait()
        halo_planes(held[n], made, at, count, parity)
        planes = pl.ds(at, count + NEAR)
        sent.append(pltpu.make_async_copy(made.at[planes], out.at[planes], sem.at[4 + n]))
        sent[-1].start()
        at += count + NEAR
    for copy in sent:
        copy.wait()


def second(x):
    return x - x.astype(BF16).astype(F32)


def fold(x, upper):
    up = jnp.where(upper, 1, 0)
    x = [x[n] for n in range(x.shape[0])]
    turned = [pltpu.roll(y, HALF_ROWS, 0) for y in x]
    row = iota(x[0].shape, 0)
    pairs = []
    for n in range(0, len(x), 2):
        later = jnp.where(up == 1, x[n], turned[n])
        sooner = jnp.where(up == 1, turned[n + 1], x[n + 1])
        pairs.append(jnp.where(row < HALF_ROWS, sooner, later))
    return pairs


def unfold(pairs, upper):
    up = jnp.where(upper, 1, 0)
    layers = []
    for y in pairs:
        turned = pltpu.roll(y, HALF_ROWS, 0)
        layers += [jnp.where(up == 1, y, turned), jnp.where(up == 1, turned, y)]
    return layers


def corner_tiles(cx):
    return cx // 2 + (cx // 2 + NEAR_CORNER) // 2


def tiles_of(x):
    return [x[n : n + 8] for n in range(0, x.shape[0], 8)]


def side_kernel(n_gy, reach, now_ref, rho_ref, last_ref, vel_ref, even_ref, *side_refs, done):
    cx, cy, nz = now_ref.shape
    i, j = lax.axis_index("gx"), lax.axis_index("gy")
    parity = lax.rem(i, 2)
    fields = (now_ref, rho_ref, last_ref, vel_ref)
    for n, side in enumerate(y_sides(n_gy)):
        row = send_row(side, j, cy, reach)
        rows = pl.ds(pl.multiple_of(row, reach), reach)
        y_ref, odd_ref, even_corner_ref = side_refs[3 * n : 3 * n + 3]
        upper = row > 0
        blocks = [[], []]
        mid = cx // 2
        for f, ref in enumerate(fields):
            y_ref[f] = ref[:, rows, :]
            for block, right in ((blocks[0], parity), (blocks[1], 1 - parity)):
                near = ref[pl.ds(mid * right, mid), rows, :]
                block += [near[m] for m in range(mid)]
                block += fold(ref[pl.ds(mid * (1 - right), mid), rows, :], upper)
                block += fold(second(ref[pl.ds((cx - NEAR_CORNER) * right, NEAR_CORNER), rows, :]), upper)
        for out_ref, block in zip((odd_ref, even_corner_ref), blocks):
            out_ref[...] = jnp.concatenate(block, axis=0).astype(BF16)
        for m in range(3):
            done(1 + 3 * n + m)
    at = 0
    for ref, count in zip(fields, plane_counts(cx)):
        halo_planes(ref, even_ref, at, count, 1 - parity)
        at += count + NEAR
    done(0)


def stage_kernel(n_gx, n_gy, steps, slots, reach, *refs):
    given, refs = refs[:8], refs[8:]
    count = 2 + 3 * len(y_sides(n_gy))
    outs, refs = refs[:count], refs[count:]
    held, made, sem = refs[:8], refs[8 : 8 + count], refs[8 + count]
    copies_in = [pltpu.make_async_copy(src, dst, sem.at[n]) for n, (src, dst) in enumerate(zip(given, held))]
    copies_out = [pltpu.make_async_copy(src, dst, sem.at[8 + n]) for n, (src, dst) in enumerate(zip(made, outs))]
    for copy in copies_in:
        copy.start()
    for copy in copies_in[:4]:
        copy.wait()
    pack_kernel(n_gx, n_gy, steps, slots, *held[:4], made[0])
    copies_out[0].start()
    for copy in copies_in[4:]:
        copy.wait()
    side_kernel(n_gy, reach, *held[4:], *made[1:], done=lambda n: copies_out[1 + n].start())
    for copy in copies_out:
        copy.wait()


def sim_kernel(n_gx, n_gy, steps, slots, reach, *refs):
    sides = y_sides(n_gy)
    fields, forward_in, arrived_in, odd_in, even_in = refs[:4], *refs[4:8]
    side_in = refs[8 : 8 + 3 * len(sides)]
    refs = refs[8 + 3 * len(sides) :]
    final_out = refs[0]
    coarse_refs, refs = (refs[1:3], refs[3:]) if n_gy == 2 else (refs[1:2], refs[2:])
    (w_ref, r_ref, prev_ref, v_ref, c0, cxu, cxd, cyu, cyd, czu, czd, inject, acc_ref), refs = refs[:13], refs[13:]
    forward_ref, arrived_ref, odd_ref, even_ref, *side_refs, sem = refs
    cx, cy, nz = fields[0].shape
    half = nz // 2
    halves = range(2)
    rows = cy + reach * len(sides)
    pad = 8
    i, j = lax.axis_index("gx"), lax.axis_index("gy")
    parity = lax.rem(i, 2)
    if n_gy == 2:
        own, halo = pad + reach * j, (pad + cy * (1 - j),)
    else:
        own, halo = pad + reach, (pad + reach + cy, pad)
    own = pl.multiple_of(own, 8)
    halo = [pl.multiple_of(at, 8) for at in halo]
    own_rows = pl.ds(own, cy)
    ext = (w_ref, r_ref, prev_ref, v_ref)
    even_base, odd_base = 2 * cx * (1 - parity), 2 * cx * parity

    copies = []

    def fetch(src, dst):
        copy = pltpu.make_async_copy(src, dst, sem.at[len(copies)])
        copy.start()
        copies.append(copy)
        return copy

    got_sensors = fetch(arrived_in, arrived_ref)
    got_fields = []
    for field, out in zip(fields, ext):
        for h in halves:
            got_fields.append(fetch(field.at[:, :, half * h : half * (h + 1)], out.at[cx : 2 * cx, h, own_rows]))
    got_halos = [fetch(odd_in, odd_ref), fetch(even_in, even_ref)]
    for n in range(len(sides)):
        own_side, even_side, odd_side = side_in[3 * n : 3 * n + 3]
        for f, out in enumerate(ext):
            for h in halves:
                src = own_side.at[f, :, :, half * h : half * (h + 1)]
                got_fields.append(fetch(src, out.at[cx : 2 * cx, h, pl.ds(halo[n], reach)]))
        got_halos.append(fetch(odd_side, side_refs[2 * n]))
        got_halos.append(fetch(even_side, side_refs[2 * n + 1]))
    got_forward = fetch(forward_in, forward_ref)

    blank = jnp.zeros((3 * cx, 2, pad, half), F32)
    for out in (w_ref, r_ref, prev_ref):
        out[:, :, 0:pad] = blank
        out[:, :, pad + rows : pad + rows + 8] = blank

    width = slots * n_gx
    per = 128 // slots
    lane = iota((8, 128), 1)

    def turned(x, turn):
        return pltpu.roll(x, turn % 128, 1) if turn % 128 else x

    def gathered(strip):
        tiles, codes = [[], [], []], []
        for g0 in range(0, n_gx, per):
            tile, code = [jnp.zeros((8, 128), F32)] * 3, jnp.zeros((8, 128), F32)
            for k in range(per):
                x = arrived_ref[g0 + k, strip]
                here = (lane >= k * slots) & (lane < (k + 1) * slots)
                for slab in range(3):
                    tile[slab] = jnp.where(here, turned(x, (k - slab) * slots), tile[slab])
                code = jnp.where(here, turned(x, (k - 3) * slots), code)
            for slab in range(3):
                tiles[slab].append(tile[slab])
            codes.append(code)
        codes = jnp.concatenate(codes, axis=1)
        return [jnp.concatenate(t, axis=1) for t in tiles], codes.astype(I32) - 1, jnp.transpose(codes).astype(I32) - 1

    def spread(cells_at, amps, column, spans, near_spans):
        depth = one_hot(iota((width, nz), 1) == (column & (nz - 1)))
        outs = []
        for part, chosen in zip(parts_of(amps, 2), (spans, near_spans)):
            block = jnp.concatenate([cells_at[a:b] * part[t : t + 1] for t, a, b in chosen], axis=0)
            outs.append(jnp.dot(block, depth, preferred_element_type=F32))
        values, first, first_near = [], 0, 0
        nearer = {t: (a, b) for t, a, b in near_spans}
        for t, a, b in spans:
            c, d = nearer[t]
            x = outs[0][first : first + b - a]
            y = x[c - a : d - a] + outs[1][first_near : first_near + d - c]
            values.append(jnp.concatenate([z for z in (x[: c - a], y, x[d - a :]) if z.shape[0]], axis=0))
            first, first_near = first + b - a, first_near + d - c
        return values

    for copy in got_fields + got_halos:
        copy.wait()
    for ref, left in ((odd_ref, 1 - parity), (even_ref, parity)):
        base = 2 * cx * (1 - left)
        at = 0
        near = base + (cx - NEAR) * left
        for out, count in zip(ext, plane_counts(cx)):
            first = base + left if count < cx else base
            for h in halves:
                lanes = slice(half * h, half * (h + 1))
                out[pl.ds(first, count), h, own_rows] = ref[at : at + count, :, lanes].astype(F32)
                out[pl.ds(near, NEAR), h, own_rows] += ref[at + count : at + count + NEAR, :, lanes].astype(F32)
            at += count + NEAR
    for n in range(len(sides)):
        upper = side_source(sides[n], j, n_gy, cy, reach)[1] > 0
        at = pl.ds(halo[n], reach)
        mid = cx // 2

        def put(out, x, tile, add=False):
            for h in halves:
                value = tile[:, half * h : half * (h + 1)]
                if add:
                    value = value + out[x, h, at]
                out[x, h, at] = value

        tall = corner_tiles(cx)
        for ref, left in ((side_refs[2 * n], 1 - parity), (side_refs[2 * n + 1], parity)):
            found = tiles_of(ref[...].astype(F32))
            base = 2 * cx * (1 - left)
            for f, out in enumerate(ext):
                tiles = found[f * tall : (f + 1) * tall]
                far = unfold(tiles[mid : mid + mid // 2], upper)
                more = unfold(tiles[mid + mid // 2 :], upper)
                for m in range(mid):
                    put(out, base + mid * left + m, tiles[m])
                    put(out, base + mid * (1 - left) + m, far[m])
                row = iota(more[0].shape, 0)
                nearer = (row >= HALF_ROWS) == upper
                for m in range(NEAR_CORNER):
                    put(out, base + (cx - NEAR_CORNER) * left + m, jnp.where(nearer, more[m], 0.0), add=True)

    got_sensors.wait()
    strips = [(j, None)]
    for side in sides:
        strip, row, there = side_source(side, j, n_gy, cy, reach)
        strips.append((strip, (row, there)))
    for n, (strip, beside) in enumerate(strips):
        amps, codes, columns = gathered(strip)
        tall = cy if beside is None else reach
        at = pl.ds(own - pad if beside is None else halo[n - 1] - pad, tall)
        for slab in range(3):
            code = codes[slab : slab + 1]
            place = code >> 8
            if beside is not None:
                y = (place & (cy - 1)) - beside[0]
                inside = (code >= 0) & (y >= 0) & (y < reach) & beside[1]
                place = jnp.where(inside, (place // cy) * reach + y, -1)
            cells = one_hot(iota((cx * tall, width), 0) == place)
            layers = [(max(t + 1 - cx * slab, 0), min(3 * cx - 1 - t - cx * slab, cx)) for t in range(steps)]
            spans = [(t, a * tall, b * tall) for t, (a, b) in enumerate(layers) if a < b]
            low, high = ((cx - NEAR) * tall, cx * tall) if slab == 0 else (0, (cx if slab == 1 else NEAR) * tall)
            near_spans = [(t, min(max(a, low), b), max(min(b, high), a)) for t, a, b in spans]
            values = spread(cells, amps[slab], columns[:, slab : slab + 1], spans, near_spans)
            for (t, a, b), value in zip(spans, values):
                value = value.reshape((b - a) // tall, tall, nz)
                xs = slice(slab * cx + a // tall, slab * cx + b // tall)
                for h in halves:
                    inject[t, xs, h, at] = value[:, :, half * h : half * (h + 1)]

    lane = iota((rows, half), 1)
    last, first = lane == half - 1, lane == 0
    mid, above, below = slice(pad, pad + rows), slice(pad + 1, pad + rows + 1), slice(pad - 1, pad + rows - 1)

    def shifted(x0, x1):
        u0, u1 = pltpu.roll(x0, half - 1, 1), pltpu.roll(x1, half - 1, 1)
        d0, d1 = pltpu.roll(x0, 1, 1), pltpu.roll(x1, 1, 1)
        return (jnp.where(last, u1, u0), u1), (d0, jnp.where(first, d0, d1))

    def over(x):
        return 2.0 / jnp.maximum(x, 1.0)

    def couple(x):
        rho = [r_ref[x, h, mid] for h in halves]
        deep, shallow = shifted(*rho)
        deep = (deep[0], jnp.where(last, 0.0, deep[1]))
        shallow = (jnp.where(first, 0.0, shallow[0]), shallow[1])
        for h in halves:
            vel = 0.11 * v_ref[x, h, mid]
            stiff = vel * vel * rho[h]
            xu, xd = stiff * over(rho[h] + r_ref[x + 1, h, mid]), stiff * over(rho[h] + r_ref[x - 1, h, mid])
            yu, yd = stiff * over(rho[h] + r_ref[x, h, above]), stiff * over(rho[h] + r_ref[x, h, below])
            zu, zd = stiff * over(rho[h] + deep[h]), stiff * over(rho[h] + shallow[h])
            c0[x, h] = 2.0 - (((xu + xd) + (yu + yd)) + (zu + zd))
            cxu[x, h], cxd[x, h], cyu[x, h], cyd[x, h] = xu, xd, yu, yd
            czu[x, h] = jnp.where(last, 0.0, zu) if h == 1 else zu
            czd[x, h] = jnp.where(first, 0.0, zd) if h == 0 else zd

    for x in range(1, 3 * cx - 1):
        couple(x)
    got_forward.wait()

    wave, prev = w_ref, prev_ref
    for t in range(steps):

        def advance(x, w, behind, wave=wave, prev=prev, t=t):
            ahead = [wave[x + 1, h, mid] for h in halves]
            deep, shallow = shifted(*w)
            for h in halves:
                u = c0[x, h] * w[h] - prev[x, h, mid] + inject[t, x, h]
                u = u + (cxu[x, h] * ahead[h] + cxd[x, h] * behind[h])
                u = u + (cyu[x, h] * wave[x, h, above] + cyd[x, h] * wave[x, h, below])
                prev[x, h, mid] = u + (czu[x, h] * deep[h] + czd[x, h] * shallow[h])
            return ahead, w

        def gather(x, prev=prev, t=t):
            for h in halves:
                term = prev[cx + x, h, own_rows] * forward_ref[t, x, :, half * h : half * (h + 1)].astype(F32)
                acc_ref[x, h] = term if t == 0 else acc_ref[x, h] + term

        at, behind = [wave[t + 1, h, mid] for h in halves], [wave[t, h, mid] for h in halves]
        for x in range(t + 1, 3 * cx - 1 - t):
            at, behind = advance(x, at, behind)
            if cx <= x < 2 * cx:
                gather(x - cx)
        wave, prev = prev, wave
    out_copies = [
        fetch(wave.at[cx : 2 * cx, h, own_rows], final_out.at[:, :, half * h : half * (h + 1)]) for h in halves
    ]

    flat = []
    for h in halves:
        blocks = []
        for a in range(0, cx, 2):
            pair = sum((-0.25 / v_ref[cx + b, h, own_rows]) * acc_ref[b, h] for b in (a, a + 1))
            blocks.append(pair)
        flat.append(jnp.concatenate(blocks, axis=0))
    if n_gy == 2:
        flat = [jnp.where(j == h, flat[0], flat[1]) for h in halves]
    half_z = one_hot(iota((half, half // 2), 0) // 2 == iota((half, half // 2), 1))
    count = cx // 2 * cy

    def half_y(tall, goal):
        return one_hot(iota((tall, count), 0) == goal(iota((tall, count), 1)))

    packed_y = half_y(count // 2, lambda at: at // 2)
    placed_y = half_y(count, lambda at: at // cy * cy + j * (cy // 2) + at % cy // 2)
    pieces = [part for h in halves for part in parts_of(flat[h], 3)[::-1]]
    depths = jnp.dot(jnp.concatenate(pieces, axis=0), half_z, preferred_element_type=F32)
    for h in halves:
        x = sum(depths[count * n : count * (n + 1)] for n in range(3 * h, 3 * h + 3))
        rows_y = placed_y if n_gy == 2 and h == 0 else packed_y
        x = sum(jnp.dot(rows_y, part, preferred_element_type=F32) for part in parts_of(x, 3)[::-1])
        if n_gy == 2:
            coarse_refs[h][...] = x.reshape(cx // 2, -1, half // 2)
        else:
            coarse_refs[0][:, half // 2 * h : half // 2 * (h + 1)] = x
    for copy in out_copies:
        copy.wait()


def call(kernel, out_shape, args, scratch=(), in_specs=None, out_specs=None, limit=60 << 20):
    return pl.pallas_call(
        kernel,
        out_shape=out_shape,
        in_specs=in_specs or [VMEM] * len(args),
        out_specs=out_specs or jax.tree.map(lambda _: VMEM, out_shape),
        scratch_shapes=scratch,
        compiler_params=pltpu.CompilerParams(vmem_limit_bytes=limit),
    )(*args)


def shards(
    n_gx,
    n_gy,
    velocity,
    density,
    adjoint_last,
    adjoint_now,
    forward_accel,
    residual_panels,
    owner_slab,
    receiver_cell,
    trace_offset,
):
    cx, cy, nz = velocity.shape
    steps = forward_accel.shape[0]
    reach = steps
    sensors = residual_panels.shape[0]
    slots = sensors // 16
    sides = y_sides(n_gy)
    shape = jax.ShapeDtypeStruct
    fields = (adjoint_now, density, adjoint_last, velocity)

    planes = sum(plane_counts(cx)) + 4 * NEAR
    halo_block = shape((planes, cy, nz), BF16)
    prep_out = [halo_block]
    for _ in sides:
        prep_out += [shape((4, cx, reach, nz), F32)] + [shape((4 * reach * corner_tiles(cx), nz), BF16)] * 2
    sensor_args = (
        residual_panels,
        owner_slab.reshape(1, sensors),
        receiver_cell.reshape(1, sensors),
        trace_offset.reshape(1, sensors),
    )
    odd_send = call(
        odd_kernel,
        halo_block,
        fields,
        [pltpu.VMEM(x.shape, x.dtype) for x in (*fields, halo_block)] + [pltpu.SemaphoreType.DMA((8,))],
        in_specs=[HBM] * 4,
        out_specs=ANY,
    )
    odd_send, *sensor_args = lax.optimization_barrier((odd_send, *sensor_args))
    stage_args = (*sensor_args, *fields)
    stage_out = [shape((n_gx, n_gy, 8, 128), F32)] + prep_out
    packed, *prep = call(
        functools.partial(stage_kernel, n_gx, n_gy, steps, slots, reach),
        stage_out,
        stage_args,
        [pltpu.VMEM(x.shape, x.dtype) for x in (*stage_args, *stage_out)] + [pltpu.SemaphoreType.DMA((32,))],
        in_specs=[HBM] * len(stage_args),
        out_specs=[ANY] * len(stage_out),
    )
    odd = [(a, a + 1) for a in range(1, n_gx - 1, 2)]
    odd = odd + [(b, a) for a, b in odd]
    even = [(a, a ^ 1) for a in range(n_gx)]
    odd_got = lax.ppermute(odd_send, "gx", odd)
    side_got = []
    for n, side in enumerate(sides):
        if side == "swap":
            over_y = [(0, 1), (1, 0)]
        elif side == "high":
            over_y = [(b + 1, b) for b in range(n_gy - 1)]
        else:
            over_y = [(b, b + 1) for b in range(n_gy - 1)]
        corner = [(a * n_gy + c, b * n_gy + d) for a, b in odd for c, d in over_y]
        own_side = lax.ppermute(prep[1 + 3 * n], "gy", over_y)
        odd_side = lax.ppermute(prep[2 + 3 * n], ("gx", "gy"), corner)
        corner = [(a * n_gy + c, b * n_gy + d) for a, b in even for c, d in over_y]
        even_side = lax.ppermute(prep[3 + 3 * n], ("gx", "gy"), corner)
        side_got.append((own_side, even_side, odd_side))
    even_got = lax.ppermute(prep[0], "gx", even)

    arrived = lax.all_to_all(
        packed.reshape(n_gx * n_gy, 8, 128), ("gx", "gy"), split_axis=0, concat_axis=0, tiled=True
    ).reshape(n_gx, n_gy, 8, 128)
    side_args = [x for got in side_got for x in got]

    rows = cy + reach * len(sides)
    padded = pltpu.VMEM((3 * cx, 2, rows + 16, nz // 2), F32)
    block = pltpu.VMEM((3 * cx, 2, rows, nz // 2), F32)
    if n_gy == 2:
        outs = [shape((cx // 2, cy, nz // 4), F32), shape((cx // 2, cy // 2, nz // 4), F32)]
    else:
        outs = [shape((cx * cy // 4, nz // 2), F32)]
    buffers = [forward_accel, arrived, odd_got, even_got] + [x for got in side_got for x in (got[2], got[1])]
    got = call(
        functools.partial(sim_kernel, n_gx, n_gy, steps, slots, reach),
        [shape((cx, cy, nz), F32)] + outs,
        fields + (forward_accel, arrived, odd_got, even_got) + tuple(side_args),
        [padded] * 4
        + [block] * 7
        + [pltpu.VMEM((steps, 3 * cx, 2, rows, nz // 2), F32), pltpu.VMEM((cx, 2, cy, nz // 2), F32)]
        + [pltpu.VMEM(x.shape, x.dtype) for x in buffers]
        + [pltpu.SemaphoreType.DMA((64,))],
        in_specs=[HBM] * 5 + [ANY] * (3 + len(side_args)),
        out_specs=[HBM] + [VMEM] * len(outs),
        limit=50 << 20,
    )
    if n_gy == 2:
        final, mine, send = got
        got = lax.ppermute(send, "gy", [(0, 1), (1, 0)])
        own_half = iota(mine.shape, 1) // (cy // 2) == lax.axis_index("gy")
        whole = jnp.where(own_half, mine, jnp.concatenate([got, got], axis=1))
        sensitivity = jnp.transpose(whole, (0, 2, 1))
    else:
        final, coarse = got
        coarse = jnp.transpose(coarse.reshape(cx // 2, cy // 2, nz // 2), (0, 2, 1))
        sensitivity = lax.all_to_all(coarse, "gy", split_axis=1, concat_axis=2, tiled=True)
    return sensitivity, final


def solution(mesh):
    in_specs = (
        P("gx", "gy", None),
        P("gx", "gy", None),
        P("gx", "gy", None),
        P("gx", "gy", None),
        P(None, "gx", "gy", None),
        P(("gx", "gy"), None),
        P(("gx", "gy"), None),
        P(("gx", "gy")),
        P(("gx", "gy")),
    )
    out_specs = (P("gx", "gy", None), P("gx", "gy", None))
    body = functools.partial(shards, mesh.shape["gx"], mesh.shape["gy"])
    return jax.shard_map(body, mesh=mesh, in_specs=in_specs, out_specs=out_specs, check_vma=False)
```
